512 devices in a mesh: mer: 64 (over y, z), grp: 2 (over x_hi), box: 4 (over x_lo, core).
Axes of the slice: x: 4 (x_hi: 2, x_lo: 2; x = x_hi * 2 + x_lo), y: 4, z: 16, core: 2. Of those that a mesh axis runs over, the one named last changes fastest.
Arguments:
- displacement: float32 [1024, 5, 5, 1024], P(('mer', 'grp', 'box')), may hold values from -0.2 to 0.2
- radius: float32 [1024, 5, 5], P(('mer', 'grp', 'box')), may hold values from 128 to 1024
- bulk_modulus: bfloat16 [1024, 5, 5, 1024], P(('mer', 'grp', 'box')), may hold values from 0.5 to 2
- inverse_mass: float32 [1024, 5, 5], P(('mer', 'grp', 'box')), may hold values from 0.5 to 2
- order_counts: int32 [1024], P(('mer', 'grp', 'box')), may hold values from 128 to 512
- source_point: int32 [65536], P(('mer', 'grp', 'box')), may hold values from 0 to 49
- route_owner: int32 [65536, 1], P(('mer', 'grp', 'box')), may hold values from 0 to 63; in each aligned block of 128 rows (0 to 127, 128 to 255, ...) at most 8 rows name the same one
- face_slot: int32 [65536], P(('mer', 'grp', 'box')), may hold values from 0 to 15
- window_start: int32 [65536], P(('mer', 'grp', 'box')), may hold values from 0 to 992
- box_field: float32 [2048, 64, 256], P('mer', 'box', 'grp'), may hold values from -6 to 6
- box_speed: float32 [2048, 64, 256], P('mer', 'box', 'grp'), may hold values from 0.25 to 1
Outputs:
- global_accel: float32 [1024, 5, 5, 1024], P(('mer', 'grp', 'box'))
- box_accel: float32 [2048, 64, 256], P('mer', 'box', 'grp')
The draws below stay inside these ranges and needn't reach their ends.
Inputs may be any that keep to these rules, and one draw needn't show every extreme that they name: `route_owner`: among the 128 records of one device no owner is named more than 8 times, a bound that some block reaches.
All inputs are finite; a program needn't handle non-finite values.
Results may differ from the reference program's by a relative error of at most 0.004.
Values may be sent and summed in bfloat16 or wider, within the bound.
A program may use at most 64 MiB of HBM per device.

```python
import math
import jax
import jax.numpy as jnp
import numpy as np
from jax import lax

NU = 512
GLL = 5
ELEM = 2
NREC = 128
CX = 32
CY = 16
NPHI = 1024
ELEMS = 1024
CAP = 8
BXN = 2048
BYN = 64
BZN = 256
N_MER = 64
N_GRP = 2
N_BOX = 4
DEVICES = 512


def with_ends(values, key, least, largest):
    extent = values.shape
    spot = [jax.random.randint(jax.random.fold_in(key, axis), (), 0, extent[axis]) for axis in range(len(extent))]
    values = values.at[tuple(spot)].set(least)
    longest = extent.index(max(extent))
    spot[longest] = (spot[longest] + 1) % extent[longest]
    return values.at[tuple(spot)].set(largest)


def shard_levels(own_key, dims, cuts, least, high):
    loudness, own = 1.0, jax.random.fold_in(own_key, 6)
    for dim, shards_of in cuts:
        draws = jnp.exp(jax.random.uniform(jax.random.fold_in(own, dim), (shards_of,), jnp.float32, least / len(cuts), high / len(cuts)))
        loudness = loudness * jnp.repeat(draws, dims[dim] // shards_of).reshape([-1 if axis == dim else 1 for axis in range(len(dims))])
    return loudness


def routed_block(own_key, own, number, rows, amount, top, bound, skew):
    sequence = jax.random.permutation(own_key, amount)
    heavy_load, ordinary = portions_of(amount, rows * top, bound, skew, True), portions_of(amount, rows * top, bound, skew, False)
    places = jnp.arange(amount)

    def named(lengths, offset_by):
        used = int((lengths > 0).sum())
        fixed = max(1, used // 4)
        passed = fixed + (places - fixed + offset_by * (used - fixed)) % max(1, amount - fixed)
        return jnp.zeros((amount,), jnp.int32).at[sequence[jnp.where(places < fixed, places, passed)]].set(jnp.asarray(lengths, jnp.int32))

    lengths = jnp.where(number % 4 == 0, named(heavy_load, number // 4), named(ordinary, number - number // 4 - 1))
    mixed = jax.random.permutation(jax.random.fold_in(own, 3), amount)
    giver, sink = mixed[0:amount // 2 * 2:2], mixed[1:amount // 2 * 2:2]
    slack = jnp.minimum(lengths[giver] - 1, bound - lengths[sink]) // 2
    slack = jnp.where((giver == sequence[0]) | (sink == sequence[0]) | (lengths[sink] == 0), 0, jnp.maximum(slack, 0))
    passed = jax.random.randint(jax.random.fold_in(own, 4), (amount // 2,), 0, 1 << 20) % (slack + 1)
    lengths = lengths.at[giver].add(-passed).at[sink].add(passed)
    items = jnp.searchsorted(jnp.cumsum(lengths), jnp.arange(rows * top), side="right").astype(jnp.int32)
    grid = items.reshape(top, rows).T
    grid = grid[jax.random.permutation(jax.random.fold_in(own, 1), rows)]
    offset_by = jax.random.randint(jax.random.fold_in(own, 2), (rows, 1), 0, top)
    return jnp.take_along_axis(grid, (jnp.arange(top)[None, :] + offset_by) % top, axis=1)


def portions_of(count, total, most, slope, full):
    loads = [(1 << 20) // math.isqrt(rank ** slope) + 1 for rank in range(1, count + 1)]
    largest = most if full else min(most, max(-(-total // count), total * loads[0] // sum(loads)))
    least = 1 if total - largest >= count - 1 else 0
    given, spare = [largest] + [least] * (count - 1), total - largest - least * (count - 1)
    while spare > 0:
        free = [i for i in range(1, count) if given[i] < largest] or [i for i in range(1, count) if given[i] < most]
        whole, left = sum([loads[i] for i in free]), spare
        for i in free:
            extra = min(most - given[i], max(1, left * loads[i] // whole), spare)
            given[i] = given[i] + extra
            spare = spare - extra
    return np.array(given)


def normal_values(stream_key, dims, scale, reach, cuts=(), kind=jnp.bfloat16):
    values = jax.random.normal(stream_key, dims, jnp.float32) * scale
    if len(cuts) > 0:
        values = shard_levels(stream_key, dims, cuts, -0.22, 0.18) * values
    return jnp.clip(values, min=-reach, max=reach).astype(kind)


def setup_inputs(seed: int = 0) -> dict:
    streams_of = jax.random.split(jax.random.key(seed), 12)
    displacement = normal_values(streams_of[0], (ELEMS, GLL, GLL, 2 * NU), 0.03, 0.2, ((0, 512),), jnp.float32)
    radius = jnp.clip(jnp.exp(math.log(1024.0) - 2.0794415 * jax.random.uniform(streams_of[1], (ELEMS, GLL, GLL), jnp.float32) ** shard_levels(streams_of[1], (ELEMS, GLL, GLL), ((0, 512),), -0.2, 0.2)), 128.0, 1024.0)
    bulk_modulus = jnp.clip(jnp.exp(math.log(2.0) - 1.3862944 * jax.random.uniform(streams_of[2], (ELEMS, GLL, GLL, NPHI), jnp.float32) ** shard_levels(streams_of[2], (ELEMS, GLL, GLL, NPHI), ((0, 512),), -0.2, 0.2)), 0.5, 2.0).astype(jnp.bfloat16)
    inverse_mass = jnp.clip(jnp.exp(math.log(2.0) - 1.3862944 * jax.random.uniform(streams_of[3], (ELEMS, GLL, GLL), jnp.float32) ** shard_levels(streams_of[3], (ELEMS, GLL, GLL), ((0, 512),), -0.2, 0.2)), 0.5, 2.0)
    order_counts = with_ends(jax.random.randint(streams_of[4], (ELEMS,), NU // 4, NU + 1), jax.random.fold_in(streams_of[4], 1), NU // 4, NU).astype(jnp.int32)
    source_point = with_ends(jax.random.randint(streams_of[5], (DEVICES * NREC,), 0, ELEM * GLL * GLL), jax.random.fold_in(streams_of[5], 1), 0, (ELEM * GLL * GLL) - 1).astype(jnp.int32)
    route_owner_keys = jax.random.split(jax.random.fold_in(streams_of[6], 1), (DEVICES * NREC) // NREC)
    route_owner_turns = jax.random.permutation(jax.random.fold_in(streams_of[6], 3), (DEVICES * NREC) // NREC)
    route_owner = jax.vmap(lambda own, number: routed_block(jax.random.fold_in(streams_of[6], 2), own, number, NREC, N_MER, 1, CAP, 2))(route_owner_keys, route_owner_turns).reshape((DEVICES * NREC, 1))
    face_slot = with_ends(jax.random.randint(streams_of[7], (DEVICES * NREC,), 0, CY), jax.random.fold_in(streams_of[7], 1), 0, CY - 1).astype(jnp.int32)
    window_start = with_ends(jax.random.randint(streams_of[8], (DEVICES * NREC,), 0, NPHI - CX + 1), jax.random.fold_in(streams_of[8], 1), 0, NPHI - CX).astype(jnp.int32)
    box_field = normal_values(streams_of[9], (BXN, BYN, BZN), 1.0, 6.0, ((0, 64), (1, 4), (2, 2)), jnp.float32)
    box_speed = jnp.clip(jnp.exp(math.log(1.0) - 1.3862944 * jax.random.uniform(streams_of[10], (BXN, BYN, BZN), jnp.float32) ** shard_levels(streams_of[10], (BXN, BYN, BZN), ((0, 64), (1, 4), (2, 2)), -0.2, 0.2)), 0.25, 1.0)
    return {"displacement": displacement, "radius": radius, "bulk_modulus": bulk_modulus, "inverse_mass": inverse_mass, "order_counts": order_counts, "source_point": source_point, "route_owner": route_owner, "face_slot": face_slot, "window_start": window_start, "box_field": box_field, "box_speed": box_speed}


TRACTION_SCALE = 0.25
HIGHEST = lax.Precision.HIGHEST

def gll_derivative():
    gll_nodes = np.array([-1.0, -math.sqrt(3.0 / 7.0), 0.0, math.sqrt(3.0 / 7.0), 1.0])
    legendre = (35.0 * gll_nodes ** 4 - 30.0 * gll_nodes ** 2 + 3.0) / 8.0
    npoints = gll_nodes.shape[0]
    degree = npoints - 1
    deriv_table = np.zeros((npoints, npoints))
    for row_index in range(npoints):
        for col_index in range(npoints):
            if row_index != col_index:
                deriv_table[row_index, col_index] = legendre[row_index] / (legendre[col_index] * (gll_nodes[row_index] - gll_nodes[col_index]))
    deriv_table[0, 0] = -degree * (degree + 1) / 4.0
    deriv_table[-1, -1] = degree * (degree + 1) / 4.0
    return deriv_table.astype(np.float32)

def azimuth_tables(orders_total):
    samples = 2 * orders_total
    order_ids = jnp.arange(orders_total, dtype=jnp.int32)
    sample_ids = jnp.arange(samples, dtype=jnp.int32)
    product = order_ids[:, None] * sample_ids[None, :] % samples
    angles = product.astype(jnp.float32) * (2.0 * math.pi / samples)
    cosine = jnp.cos(angles)
    sine = jnp.sin(angles)
    weights = jnp.where(order_ids == 0, 1.0, 2.0).astype(jnp.float32)[:, None]
    synthesis = jnp.concatenate([weights * cosine, -weights * sine], axis=0).astype(jnp.bfloat16)
    analysis = (jnp.concatenate([cosine, -sine], axis=0).T / samples).astype(jnp.bfloat16)
    return (synthesis, analysis)

def element_force(field, radius, modulus, mask, deriv, synthesis, analysis):
    orders_total = field.shape[-1] // 2
    order_vals = jnp.arange(orders_total).astype(jnp.float32)
    masked = field * mask[:, None, None, :]
    grad_first = jnp.einsum('ac,ecbk->eabk', deriv, masked, precision=HIGHEST)
    grad_second = jnp.einsum('bc,eack->eabk', deriv, masked, precision=HIGHEST)
    inverse_radius = (1.0 / radius)[..., None]
    grad_azimuth = jnp.concatenate([-order_vals * masked[..., orders_total:], order_vals * masked[..., :orders_total]], axis=-1) * inverse_radius
    gradient = jnp.stack([grad_first, grad_second, grad_azimuth]).astype(jnp.bfloat16)
    grad_shape = gradient.shape
    physical = jnp.dot(gradient.reshape(-1, grad_shape[-1]), synthesis, preferred_element_type=jnp.float32)
    physical = physical.reshape(grad_shape[:-1] + (synthesis.shape[1],))
    stress = (modulus[None].astype(jnp.float32) * physical).astype(jnp.bfloat16)
    coeffs = jnp.dot(stress.reshape(-1, stress.shape[-1]), analysis, preferred_element_type=jnp.float32)
    coeffs = coeffs.reshape(grad_shape) * mask[None, :, None, None, :]
    divergence = jnp.einsum('ca,ecbk->eabk', deriv, coeffs[0], precision=HIGHEST)
    divergence = divergence + jnp.einsum('cb,eack->eabk', deriv, coeffs[1], precision=HIGHEST)
    azimuth_part = coeffs[2]
    divergence = divergence + jnp.concatenate([order_vals * azimuth_part[..., orders_total:], -order_vals * azimuth_part[..., :orders_total]], axis=-1) * inverse_radius
    return (masked, coeffs[1], divergence)

def reference(displacement, radius, bulk_modulus, inverse_mass, order_counts, source_point, route_owner, face_slot, window_start, box_field, box_speed):
    devices = N_MER * N_GRP * N_BOX
    deriv = jnp.asarray(gll_derivative())
    synthesis, analysis = azimuth_tables(NU)
    order_ids = jnp.arange(2 * NU, dtype=jnp.int32) % NU
    mask = (order_ids[None, :] < order_counts[:, None]).astype(jnp.float32)

    def per_device(pieces):
        field, radii, modulus, mask_rows = pieces
        return element_force(field, radii, modulus, mask_rows, deriv, synthesis, analysis)
    grouped = (displacement.reshape((devices, ELEM, GLL, GLL, 2 * NU)), radius.reshape((devices, ELEM, GLL, GLL)), bulk_modulus.reshape((devices, ELEM, GLL, GLL, NPHI)), mask.reshape((devices, ELEM, 2 * NU)))
    masked, traction, divergence = lax.map(per_device, grouped)
    divergence = divergence.reshape((ELEMS, GLL, GLL, 2 * NU))
    upper_rows = divergence[:, -1]
    lower_rows = divergence[:, 0]
    zero_row = jnp.zeros_like(upper_rows[:1])
    from_below = jnp.concatenate([zero_row, upper_rows[:-1]], axis=0)
    from_above = jnp.concatenate([lower_rows[1:], zero_row], axis=0)
    assembled = divergence.at[:, 0].add(from_below).at[:, -1].add(from_above)
    global_accel = -inverse_mass[..., None] * assembled

    def synthesize(block):
        field_rows, trac_rows, points, starts = block
        coeffs = jnp.stack([field_rows[points], trac_rows[points]], axis=1).astype(jnp.bfloat16)
        synthesized = jnp.dot(coeffs.reshape(-1, 2 * NU), synthesis, preferred_element_type=jnp.float32).reshape((NREC, 2, NPHI))
        sample_index = starts[:, None, None] + jnp.arange(CX, dtype=jnp.int32)[None, None, :]
        sample_index = jnp.broadcast_to(sample_index, (NREC, 2, CX))
        return jnp.take_along_axis(synthesized, sample_index, axis=2).astype(jnp.bfloat16)
    blocks = (masked.reshape((devices, ELEM * GLL * GLL, 2 * NU)), traction.reshape((devices, ELEM * GLL * GLL, 2 * NU)), source_point.reshape((devices, NREC)), window_start.reshape((devices, NREC)))
    values = lax.map(synthesize, blocks).reshape((devices * NREC, 2, CX))
    device_ids = jnp.arange(devices * NREC, dtype=jnp.int32) // NREC
    group_ids = device_ids // N_BOX % N_GRP
    box_ids = device_ids % N_BOX
    column_ids = route_owner[:, 0][:, None] * CX + jnp.arange(CX, dtype=jnp.int32)[None, :]
    row_ids = box_ids * CY + face_slot
    faces = jnp.zeros((2, N_GRP, CX * N_MER, CY * N_BOX), jnp.float32)
    faces = faces.at[:, group_ids[:, None], column_ids, row_ids[:, None]].add(jnp.transpose(values.astype(jnp.float32), (1, 0, 2)))
    padded = jnp.pad(box_field, 1)
    padded = padded.at[1:-1, 1:-1, 0].set(faces[0, 0]).at[1:-1, 1:-1, -1].set(faces[0, N_GRP - 1])
    neighbours = padded[2:, 1:-1, 1:-1] + padded[:-2, 1:-1, 1:-1]
    neighbours = neighbours + padded[1:-1, 2:, 1:-1] + padded[1:-1, :-2, 1:-1]
    neighbours = neighbours + padded[1:-1, 1:-1, 2:] + padded[1:-1, 1:-1, :-2]
    box_accel = box_speed * (neighbours - 6.0 * box_field)
    box_accel = box_accel.at[:, :, 0].add(TRACTION_SCALE * faces[1, 0]).at[:, :, -1].add(TRACTION_SCALE * faces[1, N_GRP - 1])
    return (global_accel, box_accel)
```

```python
import functools
import math

import jax
import jax.numpy as jnp
import ml_dtypes
import numpy as np
from jax import lax
from jax.experimental import pallas as pl
from jax.experimental.pallas import tpu as pltpu
from jax.sharding import PartitionSpec as P

MESH = pl.DeviceIdType.MESH
F32 = jnp.float32
BF16 = jnp.bfloat16
NZ_FULL = 16
NREC = 128
RP = 64


def gll_derivative():
    nodes = np.array([-1.0, -math.sqrt(3.0 / 7.0), 0.0, math.sqrt(3.0 / 7.0), 1.0])
    legendre = (35.0 * nodes**4 - 30.0 * nodes**2 + 3.0) / 8.0
    table = np.zeros((5, 5))
    for i in range(5):
        for j in range(5):
            if i != j:
                table[i, j] = legendre[i] / (legendre[j] * (nodes[i] - nodes[j]))
    table[0, 0] = -5.0
    table[4, 4] = 5.0
    return table.astype(np.float32)


def split_bf16(matrix):
    hi = matrix.astype(ml_dtypes.bfloat16)
    lo = (matrix - hi.astype(np.float32)).astype(ml_dtypes.bfloat16)
    return hi, lo


def constants():
    order = np.arange(512)
    sample = np.arange(1024)
    angle = (order[:, None] * sample[None, :] % 1024) * (2.0 * math.pi / 1024)
    weight = np.where(order == 0, 1.0, 2.0)[:, None]
    synthesis = np.concatenate([weight * np.cos(angle), -weight * np.sin(angle)], 0)
    analysis = np.concatenate([np.cos(angle), -np.sin(angle)], 0).T / 1024
    synthesis = synthesis.astype(np.float32).astype(ml_dtypes.bfloat16)
    analysis = analysis.astype(np.float32).astype(ml_dtypes.bfloat16)
    deriv = gll_derivative()
    eye5, eye2 = np.eye(5, dtype=np.float32), np.eye(2, dtype=np.float32)
    d1 = np.zeros((RP, RP), np.float32)
    d2 = np.zeros((RP, RP), np.float32)
    d1[:50, :50] = np.kron(np.kron(deriv, eye5), eye2)
    d2[:50, :50] = np.kron(np.kron(eye5, deriv), eye2)
    h1, l1 = split_bf16(d1)
    h2, l2 = split_bf16(d2)
    grad = np.concatenate(
        [np.concatenate([h1, h1, l1], 1), np.concatenate([h2, h2, l2], 1)], 0
    )
    h1, l1, h2, l2 = h1.T, l1.T, h2.T, l2.T
    div = np.concatenate([h1, h2, h1, h2, l1, l2], 1)
    return synthesis[:, :512], analysis, grad, div


def dot(a, b):
    return jnp.dot(a, b, preferred_element_type=F32)


def kernel(
    ny, nz, nb,
    disp_h, rad_h, mod_h, imass_h, cnt_h, sp_h, ro_h, fs_h, ws_h, box_h, speed_h, tsyn_h, tana_h, grad_h, div_h,
    ga_h, ba_h,
    disp, rad, mod, imass, cnt, sp, ro, fs, ws, box, speed, tsyn, tana, gradm, divm,
    field, modf, radf, massf, lhs1, lhs2, pots, tracs, gather, divs, ga,
    meta, edge, edge_in, xin, yout, yin, zout, zin, vals, rhs, route, face, face_in, acc,
    in_sem, out_sem, send_sem, recv_sem,
):
    mer = lax.axis_index("mer")
    grp = lax.axis_index("grp")
    bx = lax.axis_index("box")
    my_y = mer // nz
    my_z = mer % nz
    n_mer = ny * nz
    chain = (mer * 2 + grp) * nb + bx
    n_dev = n_mer * 2 * nb

    def chain_id(d):
        d = (d + n_dev) % n_dev
        return (d // (2 * nb), (d // nb) % 2, d % nb)

    mer_up = ((mer + 1) % n_mer, grp, bx)
    mer_down = ((mer + n_mer - 1) % n_mer, grp, bx)
    box_up = (mer, grp, (bx + 1) % nb)
    box_down = (mer, grp, (bx + nb - 1) % nb)
    other = (mer, 1 - grp, bx)
    next_id = chain_id(chain + 1)
    prev_id = chain_id(chain - 1)
    y_peers = [(((my_y + k) % ny) * nz + my_z, grp, bx) for k in range(1, ny)]
    z_peers = [(my_y * nz + (my_z + k) % nz, grp, bx) for k in range(1, nz)]
    partners = [mer_up, mer_down, box_up, box_down, other, next_id, prev_id] + y_peers + z_peers

    loads = []
    for index, (src, dst) in enumerate(
        [
            (disp_h, disp), (cnt_h, cnt), (rad_h, rad), (grad_h, gradm), (tsyn_h, tsyn), (mod_h, mod), (sp_h, sp),
            (ws_h, ws), (ro_h, ro), (fs_h, fs), (box_h, box), (tana_h, tana), (div_h, divm), (speed_h, speed),
            (imass_h, imass),
        ]
    ):
        copy = pltpu.make_async_copy(src, dst, in_sem.at[index])
        copy.start()
        loads.append(copy)
    (l_disp, l_cnt, l_rad, l_grad, l_tsyn, l_mod, l_sp, l_ws, l_ro, l_fs, l_box, l_tana, l_div, l_speed, l_imass) = loads

    barrier = pltpu.get_barrier_semaphore()
    for partner in partners:
        pl.semaphore_signal(barrier, inc=1, device_id=partner, device_id_type=MESH)

    counter = [0]

    def remote(src, dst, partner):
        index = counter[0]
        counter[0] += 1
        copy = pltpu.make_async_remote_copy(
            src_ref=src, dst_ref=dst, send_sem=send_sem.at[index], recv_sem=recv_sem.at[index],
            device_id=partner, device_id_type=MESH,
        )
        copy.start()
        return copy

    lane = lax.broadcasted_iota(jnp.int32, (1, 1024), 1)
    order = lane & 511
    orderf = order.astype(F32)
    sign = (1 - 2 * (order & 1)).astype(BF16)
    row64 = lax.broadcasted_iota(jnp.int32, (RP, 1), 0)

    field[48:RP, :] = jnp.zeros((RP - 48, 1024), F32)
    radf[...] = jnp.ones((RP, 128), F32)
    l_disp.wait()
    for i in range(25):
        field[2 * i : 2 * i + 2, :] = disp[i]
    l_cnt.wait()
    counts = jnp.where((row64 & 1) == 0, cnt[0:1, 0:1], cnt[0:1, 1:2])
    mask = (order < counts).astype(F32)
    f = field[...] * mask
    l_rad.wait()
    for i in range(25):
        radf[2 * i : 2 * i + 2, :] = jnp.broadcast_to(rad[i // 5][:, i % 5 : i % 5 + 1], (2, 128))
    invr = (1.0 / radf[...])[:, 0:1]
    fhi = f.astype(BF16)
    flo = (f - fhi.astype(F32)).astype(BF16)
    l_grad.wait()
    g12 = dot(gradm[...], jnp.concatenate([fhi, flo, fhi], 0)).astype(BF16)
    lhs1[0:128, :] = g12
    lhs1[256:384, :] = g12 * sign
    g3 = (jnp.concatenate([-f[:, 512:], f[:, :512]], 1) * orderf * invr).astype(BF16)
    lhs1[128:192, :] = g3
    lhs1[384:448, :] = g3 * sign
    lhs1[192:256, :] = fhi
    lhs1[448:512, :] = fhi * sign

    l_sp.wait()
    l_ws.wait()
    second = (sp[...] >= 25).astype(jnp.int32)
    point = (sp[...] - 25 * second) * 2 + second
    packed = ((ws[...] >> 7) * RP + point) | ((ws[...] & 127) << 9)
    packed = jnp.broadcast_to(packed, (128, 128)).T
    key = packed & 511
    offset = packed >> 9
    lane128 = lax.broadcasted_iota(jnp.int32, (128, 128), 1)
    for t in range(4):
        cols = slice(t * 128, (t + 1) * 128)
        gather[0:128, cols] = (key == lane128 + t * 128).astype(F32).astype(BF16)
        gather[128:256, cols] = (key + RP == lane128 + t * 128).astype(F32).astype(BF16)

    modf[48:RP, :] = jnp.zeros((RP - 48, 1024), F32)
    l_mod.wait()
    for i in range(25):
        modf[2 * i : 2 * i + 2, :] = mod[i].astype(F32)
    l_tsyn.wait()
    for s in range(2):
        half = slice(s * 512, (s + 1) * 512)
        phys = dot(lhs1[s * 256 : (s + 1) * 256, :], tsyn[...])
        for c in range(3):
            lhs2[c * RP : (c + 1) * RP, half] = (modf[:, half] * phys[c * RP : (c + 1) * RP]).astype(BF16)
        for t in range(4):
            b = s * 4 + t
            pots[b * RP : (b + 1) * RP, :] = phys[192:256, t * 128 : (t + 1) * 128].astype(BF16)

    l_box.wait()
    yout[0:32, :] = box[pl.ds(0, 32, stride=16), :]
    yout[32:64, :] = box[pl.ds(15, 32, stride=16), :]
    far_lane = 127 * (1 - grp)
    near_lane = 127 * grp
    row128 = lax.broadcasted_iota(jnp.int32, (128, 128), 0)
    pick = (row128 == far_lane).astype(F32).astype(BF16)
    column = dot(box[...].astype(BF16), pick).reshape(64, 8, 128)
    block64 = lax.broadcasted_iota(jnp.int32, (64, 1, 128), 0)
    lane64 = lax.broadcasted_iota(jnp.int32, (64, 1, 128), 2)
    place = (block64 >> 1) + (block64 & 1) * 64
    pot_mask = lane64 == place
    trac_mask = lane64 == place + 32
    zout[...] = jnp.sum(jnp.where(pot_mask, column, 0.0), axis=0)
    l_ro.wait()
    l_fs.wait()
    meta[0] = jnp.broadcast_to(ro[...] * 16 + fs[...], (8, 128))

    pl.semaphore_wait(barrier, len(partners))
    meta_copies = [remote(meta.at[0], meta.at[k + 1], y_peers[k]) for k in range(ny - 1)]
    x_copies = [
        remote(box.at[pl.ds(0, 16)], xin.at[1], mer_down),
        remote(box.at[pl.ds(496, 16)], xin.at[0], mer_up),
    ]
    y_copies = [
        remote(yout.at[pl.ds(0, 32)], yin.at[1], box_down),
        remote(yout.at[pl.ds(32, 32)], yin.at[0], box_up),
    ]
    z_copy = remote(zout, zin, other)

    l_tana.wait()
    coeffs = dot(lhs2[...], tana[...])
    c1, c2, c3 = coeffs[0:64] * mask, coeffs[64:128] * mask, coeffs[128:192] * mask

    c2hi = c2.astype(BF16)
    synth = dot(jnp.concatenate([c2hi, c2hi * sign], 0), tsyn[...]).astype(BF16)
    for s in range(2):
        for t in range(4):
            b = s * 4 + t
            tracs[b * RP : (b + 1) * RP, :] = synth[s * RP : (s + 1) * RP, t * 128 : (t + 1) * 128]
    windows = []
    for table in (pots, tracs):
        got = dot(gather[...], table[...])
        windows.append(jnp.where(lane128 >= offset, got[0:128], got[128:256]))
    where = (offset + (lane128 & 31)) & 127
    pieces = []
    for h in range(2):
        rows = slice(h * 64, (h + 1) * 64)
        for window in windows:
            pieces.append(jnp.take_along_axis(window[rows], where[rows], axis=1, mode="promise_in_bounds"))
    quarter = lane128[0:64] >> 5
    merged = jnp.where(
        quarter == 0, pieces[0], jnp.where(quarter == 1, pieces[1], jnp.where(quarter == 2, pieces[2], pieces[3]))
    )
    vals[0] = merged.astype(BF16)
    val_copies = [remote(vals.at[0], vals.at[k + 1], y_peers[k]) for k in range(ny - 1)]

    c1hi = c1.astype(BF16)
    c1lo = (c1 - c1hi.astype(F32)).astype(BF16)
    c2lo = (c2 - c2hi.astype(F32)).astype(BF16)
    l_div.wait()
    div = dot(divm[...], jnp.concatenate([c1hi, c2hi, c1lo, c2lo, c1hi, c2hi], 0))
    div = div + jnp.concatenate([c3[:, 512:], -c3[:, :512]], 1) * orderf * invr
    divs[...] = div
    for k in range(5):
        edge[0, k : k + 1, :] = divs[41 + 2 * k : 42 + 2 * k, :]
        edge[1, k : k + 1, :] = divs[2 * k : 2 * k + 1, :]
    edge[0, 5:8, :] = jnp.zeros((3, 1024), F32)
    edge[1, 5:8, :] = jnp.zeros((3, 1024), F32)
    edge_copies = [
        remote(edge.at[0], edge_in.at[0], next_id),
        remote(edge.at[1], edge_in.at[1], prev_id),
    ]

    for copy in meta_copies:
        copy.wait_recv()
    trow = lax.broadcasted_iota(jnp.int32, (nz * 8, 128), 0)
    target = (my_y * nz + (my_z + (trow >> 3)) % nz) * 16 + (trow & 7)
    for k in range(ny):
        cols = slice(k * 128, (k + 1) * 128)
        keys = jnp.broadcast_to(meta[k][0:1, :], (nz * 8, 128))
        route[0 : nz * 8, cols] = (keys == target).astype(F32).astype(BF16)
        route[nz * 8 : nz * 16, cols] = (pltpu.roll(keys, 64, 1) == target + 8).astype(F32).astype(BF16)

    l_speed.wait()
    b = box[...]
    row512 = lax.broadcasted_iota(jnp.int32, (512, 128), 0) & 15
    lane512 = lax.broadcasted_iota(jnp.int32, (512, 128), 1)
    zero16 = jnp.zeros((16, 128), F32)
    total = jnp.concatenate([zero16, b[:-16]], 0) + jnp.concatenate([b[16:], zero16], 0)
    total = total + jnp.where(row512 == 0, 0.0, pltpu.roll(b, 1, 0)) + jnp.where(row512 == 15, 0.0, pltpu.roll(b, 511, 0))
    total = total + jnp.where(lane512 == 0, 0.0, pltpu.roll(b, 1, 1)) + jnp.where(lane512 == 127, 0.0, pltpu.roll(b, 127, 1))
    acc[...] = speed[...] * (total - 6.0 * b)

    for copy in val_copies:
        copy.wait_recv()
    for k in range(ny):
        v = vals[k].astype(F32)
        rhs[k * 128 : k * 128 + 64, :] = vals[k]
        rhs[k * 128 + 64 : (k + 1) * 128, :] = pltpu.roll(v, 64, 1).astype(BF16)
    routed = dot(route[...], rhs[...])
    face[...] = jnp.where(
        lax.broadcasted_iota(jnp.int32, (nz * 8, 128), 1) < 64, routed[: nz * 8], routed[nz * 8 :]
    ).reshape(nz, 8, 128)
    face_copies = [remote(face.at[k + 1], face_in.at[k], z_peers[k]) for k in range(nz - 1)]

    for copy in x_copies + y_copies + [z_copy]:
        copy.wait_recv()
    acc[0:16, :] += speed[0:16, :] * jnp.where(mer == 0, 0.0, xin[0])
    acc[496:512, :] += speed[496:512, :] * jnp.where(mer == n_mer - 1, 0.0, xin[1])
    acc[pl.ds(0, 32, stride=16), :] += speed[pl.ds(0, 32, stride=16), :] * jnp.where(bx == 0, 0.0, yin[0])
    acc[pl.ds(15, 32, stride=16), :] += speed[pl.ds(15, 32, stride=16), :] * jnp.where(bx == nb - 1, 0.0, yin[1])
    lane128 = lax.broadcasted_iota(jnp.int32, (128, 128), 1)
    far = (lane128 == far_lane).astype(F32).astype(BF16)
    near = (lane128 == near_lane).astype(F32).astype(BF16)
    spread = jnp.where(pot_mask, zin[...][None], 0.0).reshape(512, 128)
    acc[...] += speed[...] * dot(spread.astype(BF16), far)

    l_imass.wait()
    for i in range(25):
        massf[2 * i : 2 * i + 2, :] = jnp.broadcast_to(imass[i // 5][:, i % 5 : i % 5 + 1], (2, 128))
    for copy in edge_copies:
        copy.wait_recv()
    for k in range(5):
        inner = divs[40 + 2 * k : 41 + 2 * k, :] + divs[1 + 2 * k : 2 + 2 * k, :]
        divs[40 + 2 * k : 41 + 2 * k, :] = inner
        divs[1 + 2 * k : 2 + 2 * k, :] = inner
        divs[2 * k : 2 * k + 1, :] += jnp.where(chain == 0, 0.0, edge_in[0, k : k + 1, :])
        divs[41 + 2 * k : 42 + 2 * k, :] += jnp.where(chain == n_dev - 1, 0.0, edge_in[1, k : k + 1, :])
    for i in range(25):
        ga[i] = divs[2 * i : 2 * i + 2, :] * -massf[2 * i : 2 * i + 2, 0:1]
    ga_copy = pltpu.make_async_copy(ga, ga_h, out_sem.at[0])
    ga_copy.start()

    for copy in face_copies:
        copy.wait_recv()
    mine = face[0]
    mine = mine + jnp.sum(face_in[...], axis=0)

    def spread_face(mask):
        part = jnp.where(mask, mine[None], 0.0).reshape(512, 128)
        hi = part.astype(BF16)
        lo = (part - hi.astype(F32)).astype(BF16)
        return dot(jnp.concatenate([hi, lo], 1), jnp.concatenate([near, near], 0))

    acc[...] += speed[...] * spread_face(pot_mask) + 0.25 * spread_face(trac_mask)
    ba_copy = pltpu.make_async_copy(acc, ba_h, out_sem.at[1])
    ba_copy.start()
    for copy in meta_copies + x_copies + y_copies + [z_copy] + val_copies + edge_copies + face_copies:
        copy.wait_send()
    ga_copy.wait()
    ba_copy.wait()


def shards(ny, nz, nb, displacement, radius, bulk, imass, counts, source, owner, slot, window, box, speed):
    tsyn, tana, grad, div = constants()
    args = [
        displacement.transpose(1, 2, 0, 3).reshape(25, 2, 1024),
        radius.transpose(1, 0, 2),
        bulk.transpose(1, 2, 0, 3).reshape(25, 2, 1024),
        imass.transpose(1, 0, 2),
        counts.reshape(1, 2),
        source.reshape(1, NREC),
        owner.reshape(1, NREC),
        slot.reshape(1, NREC),
        window.reshape(1, NREC),
        box.reshape(512, 128),
        speed.reshape(512, 128),
        jnp.asarray(tsyn), jnp.asarray(tana), jnp.asarray(grad), jnp.asarray(div),
    ]
    n_copies = 2 * (ny - 1) + 5 + 2 + nz - 1
    hbm = pl.BlockSpec(memory_space=pltpu.HBM)
    vmem = pltpu.VMEM
    scratch = [vmem(a.shape, a.dtype) for a in args] + [
        vmem((RP, 1024), F32),
        vmem((RP, 1024), F32),
        vmem((RP, 128), F32),
        vmem((RP, 128), F32),
        vmem((512, 1024), BF16),
        vmem((192, 1024), BF16),
        vmem((512, 128), BF16),
        vmem((512, 128), BF16),
        vmem((256, 512), BF16),
        vmem((RP, 1024), F32),
        vmem((25, 2, 1024), F32),
        vmem((ny, 8, 128), jnp.int32),
        vmem((2, 8, 1024), F32),
        vmem((2, 8, 1024), F32),
        vmem((2, 16, 128), F32),
        vmem((64, 128), F32),
        vmem((2, 32, 128), F32),
        vmem((8, 128), F32),
        vmem((8, 128), F32),
        vmem((ny, 64, 128), BF16),
        vmem((ny * 128, 128), BF16),
        vmem((nz * 16, ny * 128), BF16),
        vmem((nz, 8, 128), F32),
        vmem((nz - 1, 8, 128), F32),
        vmem((512, 128), F32),
        pltpu.SemaphoreType.DMA((15,)),
        pltpu.SemaphoreType.DMA((2,)),
        pltpu.SemaphoreType.DMA((n_copies,)),
        pltpu.SemaphoreType.DMA((n_copies,)),
    ]
    ga, ba = pl.pallas_call(
        functools.partial(kernel, ny, nz, nb),
        out_shape=(jax.ShapeDtypeStruct((25, 2, 1024), F32), jax.ShapeDtypeStruct((512, 128), F32)),
        in_specs=[hbm] * len(args),
        out_specs=(hbm, hbm),
        scratch_shapes=scratch,
        compiler_params=pltpu.CompilerParams(
            collective_id=0, has_side_effects=True, vmem_limit_bytes=60 * 2**20
        ),
        name="step",
    )(*args)
    ga = ga.reshape(5, 5, 2, 1024).transpose(2, 0, 1, 3)
    return ga, ba.reshape(32, 16, 128)


def solution(mesh):
    n_mer = mesh.shape["mer"]
    nz = NZ_FULL if n_mer == 64 else 2
    d = P(("mer", "grp", "box"))
    return jax.shard_map(
        functools.partial(shards, n_mer // nz, nz, mesh.shape["box"]),
        mesh=mesh,
        in_specs=(d, d, d, d, d, d, d, d, d, P("mer", "box", "grp"), P("mer", "box", "grp")),
        out_specs=(d, P("mer", "box", "grp")),
        check_vma=False,
    )
```

```python
import functools
import math

import jax
import jax.numpy as jnp
import ml_dtypes
import numpy as np
from jax import lax
from jax.experimental import pallas as pl
from jax.experimental.pallas import tpu as pltpu
from jax.sharding import PartitionSpec as P

MESH = pl.DeviceIdType.MESH
F32 = jnp.float32
BF16 = jnp.bfloat16
NZ_FULL = 16
NREC = 128
RP = 64


def gll_derivative():
    nodes = np.array([-1.0, -math.sqrt(3.0 / 7.0), 0.0, math.sqrt(3.0 / 7.0), 1.0])
    legendre = (35.0 * nodes**4 - 30.0 * nodes**2 + 3.0) / 8.0
    table = np.zeros((5, 5))
    for i in range(5):
        for j in range(5):
            if i != j:
                table[i, j] = legendre[i] / (legendre[j] * (nodes[i] - nodes[j]))
    table[0, 0] = -5.0
    table[4, 4] = 5.0
    return table.astype(np.float32)


def split_bf16(matrix):
    hi = matrix.astype(ml_dtypes.bfloat16)
    lo = (matrix - hi.astype(np.float32)).astype(ml_dtypes.bfloat16)
    return hi, lo


def constants():
    order = np.arange(512)
    sample = np.arange(1024)
    angle = (order[:, None] * sample[None, :] % 1024) * (2.0 * math.pi / 1024)
    weight = np.where(order == 0, 1.0, 2.0)[:, None]
    synthesis = np.concatenate([weight * np.cos(angle), -weight * np.sin(angle)], 0)
    analysis = np.concatenate([np.cos(angle), -np.sin(angle)], 0).T / 1024
    synthesis = synthesis.astype(np.float32).astype(ml_dtypes.bfloat16)
    analysis = analysis.astype(np.float32).astype(ml_dtypes.bfloat16)
    deriv = gll_derivative()
    eye5, eye2 = np.eye(5, dtype=np.float32), np.eye(2, dtype=np.float32)
    d1 = np.zeros((RP, RP), np.float32)
    d2 = np.zeros((RP, RP), np.float32)
    d1[:50, :50] = np.kron(np.kron(deriv, eye5), eye2)
    d2[:50, :50] = np.kron(np.kron(eye5, deriv), eye2)
    h1, l1 = split_bf16(d1)
    h2, l2 = split_bf16(d2)
    grad = np.concatenate(
        [np.concatenate([h1, h1, l1], 1), np.concatenate([h2, h2, l2], 1)], 0
    )
    h1, l1, h2, l2 = h1.T, l1.T, h2.T, l2.T
    div = np.concatenate([h1, h2, h1, h2, l1, l2], 1)
    return synthesis[:, :512], analysis, grad, div


def dot(a, b):
    return jnp.dot(a, b, preferred_element_type=F32)


def kernel(
    ny, nz, nb,
    disp_h, rad_h, mod_h, imass_h, cnt_h, sp_h, ro_h, fs_h, ws_h, box_h, speed_h, tsyn_h, tana_h, grad_h, div_h,
    ga, acc,
    disp, rad, mod, imass, cnt, sp, ro, fs, ws, box, speed, tsyn, tana, gradm, divm,
    field, modf, radf, massf, lhs1, lhs2, pots, tracs, gather, divs,
    edge, edge_in, xin, yout, yin, zout, zin, vals, route, face, face_in,
    in_sem, send_sem, recv_sem,
):
    mer = lax.axis_index("mer")
    grp = lax.axis_index("grp")
    bx = lax.axis_index("box")
    my_y = mer // nz
    my_z = mer % nz
    n_mer = ny * nz
    chain = (mer * 2 + grp) * nb + bx
    n_dev = n_mer * 2 * nb

    def chain_id(d):
        d = (d + n_dev) % n_dev
        return (d // (2 * nb), (d // nb) % 2, d % nb)

    mer_up = ((mer + 1) % n_mer, grp, bx)
    mer_down = ((mer + n_mer - 1) % n_mer, grp, bx)
    box_up = (mer, grp, (bx + 1) % nb)
    box_down = (mer, grp, (bx + nb - 1) % nb)
    other = (mer, 1 - grp, bx)
    next_id = chain_id(chain + 1)
    prev_id = chain_id(chain - 1)
    ahead = sorted(
        [(dy, dz) for dy in range(ny) for dz in range(nz) if dy or dz],
        key=lambda step: (-min(step[1], nz - step[1]) - min(step[0], ny - step[0]), step),
    )
    owners = [(((my_y + dy) % ny) * nz + (my_z + dz) % nz, grp, bx) for dy, dz in ahead]
    partners = owners + [mer_up, mer_down, box_up, box_down, other, next_id, prev_id]

    barrier = pltpu.get_barrier_semaphore()
    for partner in partners:
        pl.semaphore_signal(barrier, inc=1, device_id=partner, device_id_type=MESH)

    loads = []
    for index, (src, dst) in enumerate(
        [
            (disp_h, disp), (cnt_h, cnt), (rad_h, rad), (grad_h, gradm), (tsyn_h, tsyn), (mod_h, mod), (sp_h, sp),
            (ws_h, ws), (ro_h, ro), (fs_h, fs), (box_h, box), (tana_h, tana), (div_h, divm), (speed_h, speed),
            (imass_h, imass),
        ]
    ):
        copy = pltpu.make_async_copy(src, dst, in_sem.at[index])
        copy.start()
        loads.append(copy)
    (l_disp, l_cnt, l_rad, l_grad, l_tsyn, l_mod, l_sp, l_ws, l_ro, l_fs, l_box, l_tana, l_div, l_speed, l_imass) = loads

    counter = [0]

    def remote(src, dst, partner):
        index = counter[0]
        counter[0] += 1
        copy = pltpu.make_async_remote_copy(
            src_ref=src, dst_ref=dst, send_sem=send_sem.at[index], recv_sem=recv_sem.at[index],
            device_id=partner, device_id_type=MESH,
        )
        copy.start()
        return copy

    lane = lax.broadcasted_iota(jnp.int32, (1, 1024), 1)
    order = lane & 511
    orderf = order.astype(F32)
    sign = (1 - 2 * (order & 1)).astype(BF16)
    row64 = lax.broadcasted_iota(jnp.int32, (RP, 1), 0)

    field[48:RP, :] = jnp.zeros((RP - 48, 1024), F32)
    radf[...] = jnp.ones((RP, 128), F32)
    l_disp.wait()
    for i in range(25):
        field[2 * i : 2 * i + 2, :] = disp[i]
    l_cnt.wait()
    counts = jnp.where((row64 & 1) == 0, cnt[0:1, 0:1], cnt[0:1, 1:2])
    mask = (order < counts).astype(F32)
    f = field[...] * mask
    l_rad.wait()
    for i in range(25):
        radf[2 * i : 2 * i + 2, :] = jnp.broadcast_to(rad[i // 5][:, i % 5 : i % 5 + 1], (2, 128))
    invr = (1.0 / radf[...])[:, 0:1]
    fhi = f.astype(BF16)
    flo = (f - fhi.astype(F32)).astype(BF16)
    l_grad.wait()
    g12 = dot(gradm[...], jnp.concatenate([fhi, flo, fhi], 0)).astype(BF16)
    lhs1[0:128, :] = g12
    lhs1[256:384, :] = g12 * sign
    g3 = (jnp.concatenate([-f[:, 512:], f[:, :512]], 1) * orderf * invr).astype(BF16)
    lhs1[128:192, :] = g3
    lhs1[384:448, :] = g3 * sign
    lhs1[192:256, :] = fhi
    lhs1[448:512, :] = fhi * sign

    l_sp.wait()
    l_ws.wait()
    second = (sp[...] >= 25).astype(jnp.int32)
    point = (sp[...] - 25 * second) * 2 + second
    packed = ((ws[...] >> 7) * RP + point) | ((ws[...] & 127) << 9)
    packed = jnp.broadcast_to(packed, (128, 128)).T
    key = packed & 511
    offset = packed >> 9
    lane128 = lax.broadcasted_iota(jnp.int32, (128, 128), 1)
    for t in range(4):
        cols = slice(t * 128, (t + 1) * 128)
        gather[0:128, cols] = (key == lane128 + t * 128).astype(F32).astype(BF16)
        gather[128:256, cols] = (key + RP == lane128 + t * 128).astype(F32).astype(BF16)

    l_ro.wait()
    l_fs.wait()
    row = lax.broadcasted_iota(jnp.int32, (ny * nz * 8, 128), 0)
    step = row >> 3
    target = (((my_y + step // nz) % ny) * nz + (my_z + step % nz) % nz) * 16 + (row & 7)
    keys = jnp.broadcast_to(ro[...] * 16 + fs[...], (ny * nz * 8, 128))
    route[:, 0:128] = (keys == target).astype(F32).astype(BF16)
    route[:, 128:256] = (keys == target + 8).astype(F32).astype(BF16)

    modf[48:RP, :] = jnp.zeros((RP - 48, 1024), F32)
    l_mod.wait()
    for i in range(25):
        modf[2 * i : 2 * i + 2, :] = mod[i].astype(F32)
    l_tsyn.wait()
    for s in range(2):
        half = slice(s * 512, (s + 1) * 512)
        phys = dot(lhs1[s * 256 : (s + 1) * 256, :], tsyn[...])
        for c in range(3):
            lhs2[c * RP : (c + 1) * RP, half] = (modf[:, half] * phys[c * RP : (c + 1) * RP]).astype(BF16)
        for t in range(4):
            b = s * 4 + t
            pots[b * RP : (b + 1) * RP, :] = phys[192:256, t * 128 : (t + 1) * 128].astype(BF16)

    l_box.wait()
    yout[0:32, :] = box[pl.ds(0, 32, stride=16), :]
    yout[32:64, :] = box[pl.ds(15, 32, stride=16), :]
    far_lane = 127 * (1 - grp)
    near_lane = 127 * grp
    row128 = lax.broadcasted_iota(jnp.int32, (128, 128), 0)
    pick = (row128 == far_lane).astype(F32).astype(BF16)
    column = dot(box[...].astype(BF16), pick).reshape(64, 8, 128)
    block64 = lax.broadcasted_iota(jnp.int32, (64, 1, 128), 0)
    lane64 = lax.broadcasted_iota(jnp.int32, (64, 1, 128), 2)
    place = (block64 >> 1) + (block64 & 1) * 64
    pot_mask = lane64 == place
    trac_mask = lane64 == place + 32
    zout[...] = jnp.sum(jnp.where(pot_mask, column, 0.0), axis=0)
    l_tana.wait()
    coeffs = dot(lhs2[...], tana[...])
    c1, c2, c3 = coeffs[0:64] * mask, coeffs[64:128] * mask, coeffs[128:192] * mask

    c2hi = c2.astype(BF16)
    synth = dot(jnp.concatenate([c2hi, c2hi * sign], 0), tsyn[...]).astype(BF16)
    for s in range(2):
        for t in range(4):
            b = s * 4 + t
            tracs[b * RP : (b + 1) * RP, :] = synth[s * RP : (s + 1) * RP, t * 128 : (t + 1) * 128]
    windows = []
    for table in (pots, tracs):
        got = dot(gather[...], table[...])
        windows.append(jnp.where(lane128 >= offset, got[0:128], got[128:256]))
    where = (offset + (lane128 & 31)) & 127
    pieces = [jnp.take_along_axis(window, where, axis=1, mode="promise_in_bounds") for window in windows]
    merged = jnp.where((lane128 & 32) == 0, pieces[0], pieces[1])
    vals[0:128, :] = jnp.where(lane128 < 64, merged, 0.0).astype(BF16)
    vals[128:256, :] = jnp.where(lane128 < 64, 0.0, merged).astype(BF16)
    face[...] = dot(route[...], vals[...]).reshape(ny * nz, 8, 128).astype(BF16)
    pl.semaphore_wait(barrier, len(partners))
    face_copies = [
        remote(face.at[dy * nz + dz], face_in.at[k], owners[k]) for k, (dy, dz) in enumerate(ahead)
    ]
    x_copies = [
        remote(box.at[pl.ds(0, 16)], xin.at[1], mer_down),
        remote(box.at[pl.ds(496, 16)], xin.at[0], mer_up),
    ]
    y_copies = [
        remote(yout.at[pl.ds(0, 32)], yin.at[1], box_down),
        remote(yout.at[pl.ds(32, 32)], yin.at[0], box_up),
    ]
    z_copy = remote(zout, zin, other)

    c1hi = c1.astype(BF16)
    c1lo = (c1 - c1hi.astype(F32)).astype(BF16)
    c2lo = (c2 - c2hi.astype(F32)).astype(BF16)
    l_div.wait()
    div = dot(divm[...], jnp.concatenate([c1hi, c2hi, c1lo, c2lo, c1hi, c2hi], 0))
    div = div + jnp.concatenate([c3[:, 512:], -c3[:, :512]], 1) * orderf * invr
    divs[...] = div
    for k in range(5):
        edge[0, k : k + 1, :] = divs[41 + 2 * k : 42 + 2 * k, :]
        edge[1, k : k + 1, :] = divs[2 * k : 2 * k + 1, :]
    edge[0, 5:8, :] = jnp.zeros((3, 1024), F32)
    edge[1, 5:8, :] = jnp.zeros((3, 1024), F32)
    edge_copies = [
        remote(edge.at[0], edge_in.at[0], next_id),
        remote(edge.at[1], edge_in.at[1], prev_id),
    ]

    l_speed.wait()
    b = box[...]
    row512 = lax.broadcasted_iota(jnp.int32, (512, 128), 0) & 15
    lane512 = lax.broadcasted_iota(jnp.int32, (512, 128), 1)
    zero16 = jnp.zeros((16, 128), F32)
    total = jnp.concatenate([zero16, b[:-16]], 0) + jnp.concatenate([b[16:], zero16], 0)
    total = total + jnp.where(row512 == 0, 0.0, pltpu.roll(b, 1, 0)) + jnp.where(row512 == 15, 0.0, pltpu.roll(b, 511, 0))
    total = total + jnp.where(lane512 == 0, 0.0, pltpu.roll(b, 1, 1)) + jnp.where(lane512 == 127, 0.0, pltpu.roll(b, 127, 1))
    acc[...] = speed[...] * (total - 6.0 * b)

    for copy in x_copies + y_copies + [z_copy]:
        copy.wait_recv()
    acc[0:16, :] += speed[0:16, :] * jnp.where(mer == 0, 0.0, xin[0])
    acc[496:512, :] += speed[496:512, :] * jnp.where(mer == n_mer - 1, 0.0, xin[1])
    acc[pl.ds(0, 32, stride=16), :] += speed[pl.ds(0, 32, stride=16), :] * jnp.where(bx == 0, 0.0, yin[0])
    acc[pl.ds(15, 32, stride=16), :] += speed[pl.ds(15, 32, stride=16), :] * jnp.where(bx == nb - 1, 0.0, yin[1])
    lane128 = lax.broadcasted_iota(jnp.int32, (128, 128), 1)
    far = (lane128 == far_lane).astype(F32).astype(BF16)
    near = (lane128 == near_lane).astype(F32).astype(BF16)
    spread = jnp.where(pot_mask, zin[...][None], 0.0).reshape(512, 128)
    acc[...] += speed[...] * dot(spread.astype(BF16), far)

    l_imass.wait()
    for i in range(25):
        massf[2 * i : 2 * i + 2, :] = jnp.broadcast_to(imass[i // 5][:, i % 5 : i % 5 + 1], (2, 128))
    for copy in edge_copies:
        copy.wait_recv()
    for k in range(5):
        inner = divs[40 + 2 * k : 41 + 2 * k, :] + divs[1 + 2 * k : 2 + 2 * k, :]
        divs[40 + 2 * k : 41 + 2 * k, :] = inner
        divs[1 + 2 * k : 2 + 2 * k, :] = inner
        divs[2 * k : 2 * k + 1, :] += jnp.where(chain == 0, 0.0, edge_in[0, k : k + 1, :])
        divs[41 + 2 * k : 42 + 2 * k, :] += jnp.where(chain == n_dev - 1, 0.0, edge_in[1, k : k + 1, :])
    for i in range(25):
        ga[i] = divs[2 * i : 2 * i + 2, :] * -massf[2 * i : 2 * i + 2, 0:1]

    for copy in face_copies:
        copy.wait_recv()
    mine = face[0].astype(F32) + jnp.sum(face_in[...].astype(F32), axis=0)

    def spread_face(mask):
        part = jnp.where(mask, mine[None], 0.0).reshape(512, 128)
        hi = part.astype(BF16)
        lo = (part - hi.astype(F32)).astype(BF16)
        return dot(jnp.concatenate([hi, lo], 1), jnp.concatenate([near, near], 0))

    acc[...] += speed[...] * spread_face(pot_mask) + 0.25 * spread_face(trac_mask)
    for copy in x_copies + y_copies + [z_copy] + edge_copies + face_copies:
        copy.wait_send()


def write_out(ga, ba, ga_h, ba_h, sem):
    copies = [pltpu.make_async_copy(ga, ga_h, sem.at[0]), pltpu.make_async_copy(ba, ba_h, sem.at[1])]
    for copy in copies:
        copy.start()
    for copy in copies:
        copy.wait()


def shards(ny, nz, nb, displacement, radius, bulk, imass, counts, source, owner, slot, window, box, speed):
    tsyn, tana, grad, div = constants()
    args = [
        displacement.transpose(1, 2, 0, 3).reshape(25, 2, 1024),
        radius.transpose(1, 0, 2),
        bulk.transpose(1, 2, 0, 3).reshape(25, 2, 1024),
        imass.transpose(1, 0, 2),
        counts.reshape(1, 2),
        source.reshape(1, NREC),
        owner.reshape(1, NREC),
        slot.reshape(1, NREC),
        window.reshape(1, NREC),
        box.reshape(512, 128),
        speed.reshape(512, 128),
        jnp.asarray(tsyn), jnp.asarray(tana), jnp.asarray(grad), jnp.asarray(div),
    ]
    n_copies = 5 + 2 + ny * nz - 1
    hbm = pl.BlockSpec(memory_space=pltpu.HBM)
    vmem = pltpu.VMEM
    scratch = [vmem(a.shape, a.dtype) for a in args] + [
        vmem((RP, 1024), F32),
        vmem((RP, 1024), F32),
        vmem((RP, 128), F32),
        vmem((RP, 128), F32),
        vmem((512, 1024), BF16),
        vmem((192, 1024), BF16),
        vmem((512, 128), BF16),
        vmem((512, 128), BF16),
        vmem((256, 512), BF16),
        vmem((RP, 1024), F32),
        vmem((2, 8, 1024), F32),
        vmem((2, 8, 1024), F32),
        vmem((2, 16, 128), F32),
        vmem((64, 128), F32),
        vmem((2, 32, 128), F32),
        vmem((8, 128), F32),
        vmem((8, 128), F32),
        vmem((256, 128), BF16),
        vmem((ny * nz * 8, 256), BF16),
        vmem((ny * nz, 8, 128), BF16),
        vmem((ny * nz - 1, 8, 128), BF16),
        pltpu.SemaphoreType.DMA((15,)),
        pltpu.SemaphoreType.DMA((n_copies,)),
        pltpu.SemaphoreType.DMA((n_copies,)),
    ]
    ga, ba = pl.pallas_call(
        functools.partial(kernel, ny, nz, nb),
        out_shape=(vmem((25, 2, 1024), F32), vmem((512, 128), F32)),
        in_specs=[hbm] * len(args),
        out_specs=(pl.BlockSpec(memory_space=vmem),) * 2,
        scratch_shapes=scratch,
        compiler_params=pltpu.CompilerParams(
            collective_id=0, has_side_effects=True, vmem_limit_bytes=40 * 2**20
        ),
        name="step",
    )(*[pltpu.with_memory_space_constraint(a, pltpu.HBM) for a in args])
    ga, ba = pl.pallas_call(
        write_out,
        out_shape=(jax.ShapeDtypeStruct((25, 2, 1024), F32), jax.ShapeDtypeStruct((512, 128), F32)),
        in_specs=[pl.BlockSpec(memory_space=vmem)] * 2,
        out_specs=(hbm, hbm),
        scratch_shapes=[pltpu.SemaphoreType.DMA((2,))],
        name="write_out",
    )(pltpu.with_memory_space_constraint(ga, vmem), pltpu.with_memory_space_constraint(ba, vmem))
    ga = ga.reshape(5, 5, 2, 1024).transpose(2, 0, 1, 3)
    return ga, ba.reshape(32, 16, 128)


def solution(mesh):
    n_mer = mesh.shape["mer"]
    nz = NZ_FULL if n_mer == 64 else 2
    d = P(("mer", "grp", "box"))
    return jax.shard_map(
        functools.partial(shards, n_mer // nz, nz, mesh.shape["box"]),
        mesh=mesh,
        in_specs=(d, d, d, d, d, d, d, d, d, P("mer", "box", "grp"), P("mer", "box", "grp")),
        out_specs=(d, P("mer", "box", "grp")),
        check_vma=False,
    )
```

```python
import functools
import math

import jax
import jax.numpy as jnp
import ml_dtypes
import numpy as np
from jax import lax
from jax.experimental import pallas as pl
from jax.experimental.pallas import tpu as pltpu
from jax.sharding import PartitionSpec as P

MESH = pl.DeviceIdType.MESH
F32 = jnp.float32
BF16 = jnp.bfloat16
NZ_FULL = 16
NREC = 128
RP = 64


def gll_derivative():
    nodes = np.array([-1.0, -math.sqrt(3.0 / 7.0), 0.0, math.sqrt(3.0 / 7.0), 1.0])
    legendre = (35.0 * nodes**4 - 30.0 * nodes**2 + 3.0) / 8.0
    table = np.zeros((5, 5))
    for i in range(5):
        for j in range(5):
            if i != j:
                table[i, j] = legendre[i] / (legendre[j] * (nodes[i] - nodes[j]))
    table[0, 0] = -5.0
    table[4, 4] = 5.0
    return table.astype(np.float32)


def split_bf16(matrix):
    hi = matrix.astype(ml_dtypes.bfloat16)
    lo = (matrix - hi.astype(np.float32)).astype(ml_dtypes.bfloat16)
    return hi, lo


def constants():
    order = np.arange(512)
    sample = np.arange(1024)
    angle = (order[:, None] * sample[None, :] % 1024) * (2.0 * math.pi / 1024)
    weight = np.where(order == 0, 1.0, 2.0)[:, None]
    synthesis = np.concatenate([weight * np.cos(angle), -weight * np.sin(angle)], 0)
    analysis = np.concatenate([np.cos(angle), -np.sin(angle)], 0).T / 1024
    synthesis = synthesis.astype(np.float32).astype(ml_dtypes.bfloat16)
    analysis = analysis.astype(np.float32).astype(ml_dtypes.bfloat16)
    deriv = gll_derivative()
    eye5, eye2 = np.eye(5, dtype=np.float32), np.eye(2, dtype=np.float32)
    d1 = np.zeros((RP, RP), np.float32)
    d2 = np.zeros((RP, RP), np.float32)
    d1[:50, :50] = np.kron(np.kron(deriv, eye5), eye2)
    d2[:50, :50] = np.kron(np.kron(eye5, deriv), eye2)
    h1, l1 = split_bf16(d1)
    h2, l2 = split_bf16(d2)
    grad = np.concatenate(
        [np.concatenate([h1, h1, l1], 1), np.concatenate([h2, h2, l2], 1)], 0
    )
    h1, l1, h2, l2 = h1.T, l1.T, h2.T, l2.T
    div = np.concatenate([h1, h2, h1, h2, l1, l2], 1)
    return synthesis[:, :512], analysis, grad, div


def dot(a, b):
    return jnp.dot(a, b, preferred_element_type=F32)


def kernel(
    ny, nz, nb,
    disp_h, rad_h, mod_h, imass_h, cnt_h, sp_h, ro_h, fs_h, ws_h, box_h, speed_h, tsyn_h, tana_h, grad_h, div_h,
    ga, acc,
    disp, rad, mod, imass, cnt, sp, ro, fs, ws, box, speed, tsyn, tana, gradm, divm,
    field, modf, radf, massf, lhs1, lhs2, pots, tracs, gather, divs,
    edge, edge_in, xin, yout, yin, zout, zin, spot, vals, route, part_in, line, face, face_in,
    in_sem, send_sem, recv_sem, relay_sem,
):
    mer = lax.axis_index("mer")
    grp = lax.axis_index("grp")
    bx = lax.axis_index("box")
    my_y = mer // nz
    my_z = mer % nz
    n_mer = ny * nz
    chain = (mer * 2 + grp) * nb + bx
    n_dev = n_mer * 2 * nb

    def chain_id(d):
        d = (d + n_dev) % n_dev
        return (d // (2 * nb), (d // nb) % 2, d % nb)

    mer_up = ((mer + 1) % n_mer, grp, bx)
    mer_down = ((mer + n_mer - 1) % n_mer, grp, bx)
    box_up = (mer, grp, (bx + 1) % nb)
    box_down = (mer, grp, (bx + nb - 1) % nb)
    other = (mer, 1 - grp, bx)
    next_id = chain_id(chain + 1)
    prev_id = chain_id(chain - 1)
    y_ahead = sorted(range(1, ny), key=lambda k: (-min(k, ny - k), k))
    z_ahead = sorted(range(1, nz), key=lambda k: (-min(k, nz - k), k))
    y_peers = [(((my_y + k) % ny) * nz + my_z, grp, bx) for k in y_ahead]
    z_peers = [(my_y * nz + (my_z + k) % nz, grp, bx) for k in z_ahead]
    reach = nz // 4
    relay_up = (my_y * nz + (my_z + reach) % nz, grp, bx)
    relay_down = (my_y * nz + (my_z + nz - reach) % nz, grp, bx)
    z_near = [z_peers[i] for i, k in enumerate(z_ahead) if min(k, nz - k) <= reach]
    partners = z_near + y_peers + [mer_up, mer_down, box_up, box_down, other, next_id, prev_id]

    barrier = pltpu.get_barrier_semaphore()
    for partner in partners:
        pl.semaphore_signal(barrier, inc=1, device_id=partner, device_id_type=MESH)

    loads = []
    for index, (src, dst) in enumerate(
        [
            (disp_h, disp), (cnt_h, cnt), (rad_h, rad), (grad_h, gradm), (tsyn_h, tsyn), (mod_h, mod), (sp_h, sp),
            (ws_h, ws), (ro_h, ro), (fs_h, fs), (box_h, box), (tana_h, tana), (div_h, divm), (speed_h, speed),
            (imass_h, imass),
        ]
    ):
        copy = pltpu.make_async_copy(src, dst, in_sem.at[index])
        copy.start()
        loads.append(copy)
    (l_disp, l_cnt, l_rad, l_grad, l_tsyn, l_mod, l_sp, l_ws, l_ro, l_fs, l_box, l_tana, l_div, l_speed, l_imass) = loads

    counter = [0]

    def remote(src, dst, partner):
        index = counter[0]
        counter[0] += 1
        copy = pltpu.make_async_remote_copy(
            src_ref=src, dst_ref=dst, send_sem=send_sem.at[index], recv_sem=recv_sem.at[index],
            device_id=partner, device_id_type=MESH,
        )
        copy.start()
        return copy

    lane = lax.broadcasted_iota(jnp.int32, (1, 1024), 1)
    order = lane & 511
    orderf = order.astype(F32)
    sign = (1 - 2 * (order & 1)).astype(BF16)
    row64 = lax.broadcasted_iota(jnp.int32, (RP, 1), 0)

    field[48:RP, :] = jnp.zeros((RP - 48, 1024), F32)
    radf[...] = jnp.ones((RP, 128), F32)
    l_disp.wait()
    for i in range(25):
        field[2 * i : 2 * i + 2, :] = disp[i]
    l_cnt.wait()
    counts = jnp.where((row64 & 1) == 0, cnt[0:1, 0:1], cnt[0:1, 1:2])
    mask = (order < counts).astype(F32)
    f = field[...] * mask
    l_rad.wait()
    for i in range(25):
        radf[2 * i : 2 * i + 2, :] = jnp.broadcast_to(rad[i // 5][:, i % 5 : i % 5 + 1], (2, 128))
    invr = (1.0 / radf[...])[:, 0:1]
    fhi = f.astype(BF16)
    flo = (f - fhi.astype(F32)).astype(BF16)
    l_grad.wait()
    g12 = dot(gradm[...], jnp.concatenate([fhi, flo, fhi], 0)).astype(BF16)
    lhs1[0:128, :] = g12
    lhs1[256:384, :] = g12 * sign
    g3 = (jnp.concatenate([-f[:, 512:], f[:, :512]], 1) * orderf * invr).astype(BF16)
    lhs1[128:192, :] = g3
    lhs1[384:448, :] = g3 * sign
    lhs1[192:256, :] = fhi
    lhs1[448:512, :] = fhi * sign

    l_sp.wait()
    l_ws.wait()
    second = (sp[...] >= 25).astype(jnp.int32)
    point = (sp[...] - 25 * second) * 2 + second
    packed = ((ws[...] >> 7) * RP + point) | ((ws[...] & 127) << 9)
    packed = jnp.broadcast_to(packed, (128, 128)).T
    key = packed & 511
    offset = packed >> 9
    lane128 = lax.broadcasted_iota(jnp.int32, (128, 128), 1)
    for t in range(4):
        cols = slice(t * 128, (t + 1) * 128)
        gather[0:128, cols] = (key == lane128 + t * 128).astype(F32).astype(BF16)
        gather[128:256, cols] = (key + RP == lane128 + t * 128).astype(F32).astype(BF16)

    l_ro.wait()
    l_fs.wait()
    row = lax.broadcasted_iota(jnp.int32, (ny * nz * 8, 128), 0)
    step = row >> 3
    target = (((my_y + step // nz) % ny) * nz + (my_z + step % nz) % nz) * 16 + (row & 7)
    keys = jnp.broadcast_to(ro[...] * 16 + fs[...], (ny * nz * 8, 128))
    route[:, 0:128] = (keys == target).astype(F32).astype(BF16)
    route[:, 128:256] = (keys == target + 8).astype(F32).astype(BF16)

    modf[48:RP, :] = jnp.zeros((RP - 48, 1024), F32)
    l_mod.wait()
    for i in range(25):
        modf[2 * i : 2 * i + 2, :] = mod[i].astype(F32)
    l_tsyn.wait()
    for s in range(2):
        half = slice(s * 512, (s + 1) * 512)
        phys = dot(lhs1[s * 256 : (s + 1) * 256, :], tsyn[...])
        for c in range(3):
            lhs2[c * RP : (c + 1) * RP, half] = (modf[:, half] * phys[c * RP : (c + 1) * RP]).astype(BF16)
        for t in range(4):
            b = s * 4 + t
            pots[b * RP : (b + 1) * RP, :] = phys[192:256, t * 128 : (t + 1) * 128].astype(BF16)

    l_box.wait()
    yout[0:32, :] = box[pl.ds(0, 32, stride=16), :]
    yout[32:64, :] = box[pl.ds(15, 32, stride=16), :]
    far_lane = 127 * (1 - grp)
    near_lane = 127 * grp
    row128 = lax.broadcasted_iota(jnp.int32, (128, 128), 0)
    pick = (row128 == far_lane).astype(F32).astype(BF16)
    column = dot(box[...].astype(BF16), pick).reshape(64, 8, 128)
    block64 = lax.broadcasted_iota(jnp.int32, (64, 1, 128), 0)
    lane64 = lax.broadcasted_iota(jnp.int32, (64, 1, 128), 2)
    place = (block64 >> 1) + (block64 & 1) * 64
    pot_mask = lane64 == place
    trac_mask = lane64 == place + 32
    zout[...] = jnp.sum(jnp.where(pot_mask, column, 0.0), axis=0)
    l_tana.wait()
    coeffs = dot(lhs2[...], tana[...])
    c1, c2, c3 = coeffs[0:64] * mask, coeffs[64:128] * mask, coeffs[128:192] * mask

    c2hi = c2.astype(BF16)
    synth = dot(jnp.concatenate([c2hi, c2hi * sign], 0), tsyn[...]).astype(BF16)
    for s in range(2):
        for t in range(4):
            b = s * 4 + t
            tracs[b * RP : (b + 1) * RP, :] = synth[s * RP : (s + 1) * RP, t * 128 : (t + 1) * 128]
    windows = []
    for table in (pots, tracs):
        got = dot(gather[...], table[...])
        windows.append(jnp.where(lane128 >= offset, got[0:128], got[128:256]))
    where = (offset + (lane128 & 31)) & 127
    pieces = [jnp.take_along_axis(window, where, axis=1, mode="promise_in_bounds") for window in windows]
    merged = jnp.where((lane128 & 32) == 0, pieces[0], pieces[1])
    vals[0:128, :] = jnp.where(lane128 < 64, merged, 0.0).astype(BF16)
    vals[128:256, :] = jnp.where(lane128 < 64, 0.0, merged).astype(BF16)
    face[...] = dot(route[...], vals[...]).reshape(ny * nz, 8, 128).astype(BF16)
    pl.semaphore_wait(barrier, len(partners))
    pl.semaphore_signal(relay_sem.at[0], inc=1, device_id=relay_up, device_id_type=MESH)
    pl.semaphore_signal(relay_sem.at[1], inc=1, device_id=relay_down, device_id_type=MESH)
    part_copies = [
        remote(face.at[pl.ds(step * nz, nz)], part_in.at[k], y_peers[k]) for k, step in enumerate(y_ahead)
    ]
    x_copies = [
        remote(box.at[pl.ds(0, 16)], xin.at[1], mer_down),
        remote(box.at[pl.ds(496, 16)], xin.at[0], mer_up),
    ]
    y_copies = [
        remote(yout.at[pl.ds(0, 32)], yin.at[1], box_down),
        remote(yout.at[pl.ds(32, 32)], yin.at[0], box_up),
    ]
    z_copy = remote(zout, zin, other)

    c1hi = c1.astype(BF16)
    c1lo = (c1 - c1hi.astype(F32)).astype(BF16)
    c2lo = (c2 - c2hi.astype(F32)).astype(BF16)
    l_div.wait()
    div = dot(divm[...], jnp.concatenate([c1hi, c2hi, c1lo, c2lo, c1hi, c2hi], 0))
    div = div + jnp.concatenate([c3[:, 512:], -c3[:, :512]], 1) * orderf * invr
    divs[...] = div
    for k in range(5):
        edge[0, k : k + 1, :] = divs[41 + 2 * k : 42 + 2 * k, :]
        edge[1, k : k + 1, :] = divs[2 * k : 2 * k + 1, :]
    edge[0, 5:8, :] = jnp.zeros((3, 1024), F32)
    edge[1, 5:8, :] = jnp.zeros((3, 1024), F32)
    edge_copies = [
        remote(edge.at[0], edge_in.at[0], next_id),
        remote(edge.at[1], edge_in.at[1], prev_id),
    ]

    l_speed.wait()
    b = box[...]
    row512 = lax.broadcasted_iota(jnp.int32, (512, 128), 0) & 15
    lane512 = lax.broadcasted_iota(jnp.int32, (512, 128), 1)
    zero16 = jnp.zeros((16, 128), F32)
    total = jnp.concatenate([zero16, b[:-16]], 0) + jnp.concatenate([b[16:], zero16], 0)
    total = total + jnp.where(row512 == 0, 0.0, pltpu.roll(b, 1, 0)) + jnp.where(row512 == 15, 0.0, pltpu.roll(b, 511, 0))
    total = total + jnp.where(lane512 == 0, 0.0, pltpu.roll(b, 1, 1)) + jnp.where(lane512 == 127, 0.0, pltpu.roll(b, 127, 1))
    acc[...] = speed[...] * (total - 6.0 * b)

    part = face[0:nz].astype(F32)
    for k, copy in enumerate(part_copies):
        copy.wait_recv()
        part = part + part_in[k].astype(F32)
    line[...] = part.astype(BF16)
    pl.semaphore_wait(relay_sem.at[0], 1)
    pl.semaphore_wait(relay_sem.at[1], 1)
    face_copies = [remote(line.at[step], face_in.at[k], z_peers[k]) for k, step in enumerate(z_ahead)]

    for copy in x_copies + y_copies + [z_copy]:
        copy.wait_recv()
    acc[0:16, :] += speed[0:16, :] * jnp.where(mer == 0, 0.0, xin[0])
    acc[496:512, :] += speed[496:512, :] * jnp.where(mer == n_mer - 1, 0.0, xin[1])
    acc[pl.ds(0, 32, stride=16), :] += speed[pl.ds(0, 32, stride=16), :] * jnp.where(bx == 0, 0.0, yin[0])
    acc[pl.ds(15, 32, stride=16), :] += speed[pl.ds(15, 32, stride=16), :] * jnp.where(bx == nb - 1, 0.0, yin[1])
    lane128 = lax.broadcasted_iota(jnp.int32, (128, 128), 1)
    far = (lane128 == far_lane).astype(F32).astype(BF16)
    spread = jnp.where(pot_mask, zin[...][None], 0.0).reshape(512, 128)
    acc[...] += speed[...] * dot(spread.astype(BF16), far)

    l_imass.wait()
    for i in range(25):
        massf[2 * i : 2 * i + 2, :] = jnp.broadcast_to(imass[i // 5][:, i % 5 : i % 5 + 1], (2, 128))
    for copy in edge_copies:
        copy.wait_recv()
    for k in range(5):
        inner = divs[40 + 2 * k : 41 + 2 * k, :] + divs[1 + 2 * k : 2 + 2 * k, :]
        divs[40 + 2 * k : 41 + 2 * k, :] = inner
        divs[1 + 2 * k : 2 + 2 * k, :] = inner
        divs[2 * k : 2 * k + 1, :] += jnp.where(chain == 0, 0.0, edge_in[0, k : k + 1, :])
        divs[41 + 2 * k : 42 + 2 * k, :] += jnp.where(chain == n_dev - 1, 0.0, edge_in[1, k : k + 1, :])
    for i in range(25):
        ga[i] = divs[2 * i : 2 * i + 2, :] * -massf[2 * i : 2 * i + 2, 0:1]

    both_mask = pot_mask | trac_mask
    row256 = lax.broadcasted_iota(jnp.int32, (256, 256), 0)
    col256 = lax.broadcasted_iota(jnp.int32, (256, 256), 1)
    keep = ((row256 & 32) == 0) == (col256 < 128)
    spot[...] = (keep & ((col256 & 127) == near_lane)).astype(F32).astype(BF16)
    for copy in x_copies + y_copies + [z_copy] + part_copies + edge_copies + face_copies:
        copy.wait_send()
    cut = len(face_copies) // 2
    mine = part[0]
    for first, last in ((cut, len(face_copies)), (0, cut)):
        if first < last:
            for k in range(last - 1, first - 1, -1):
                face_copies[k].wait_recv()
            mine = mine + jnp.sum(face_in[first:last].astype(F32), axis=0)
    hi = mine.astype(BF16).astype(F32)
    lo = mine - hi
    hi = jnp.where(both_mask, hi[None], 0.0).reshape(512, 128).astype(BF16)
    lo = jnp.where(both_mask, lo[None], 0.0).reshape(512, 128).astype(BF16)
    sides = dot(jnp.concatenate([hi, lo], 1), spot[...])
    acc[...] += speed[...] * sides[:, :128] + 0.25 * sides[:, 128:]


def write_out(ga, ba, ga_h, ba_h, sem):
    copies = [pltpu.make_async_copy(ga, ga_h, sem.at[0]), pltpu.make_async_copy(ba, ba_h, sem.at[1])]
    for copy in copies:
        copy.start()
    for copy in copies:
        copy.wait()


def shards(ny, nz, nb, displacement, radius, bulk, imass, counts, source, owner, slot, window, box, speed):
    tsyn, tana, grad, div = constants()
    args = [
        displacement.transpose(1, 2, 0, 3).reshape(25, 2, 1024),
        radius.transpose(1, 0, 2),
        bulk.transpose(1, 2, 0, 3).reshape(25, 2, 1024),
        imass.transpose(1, 0, 2),
        counts.reshape(1, 2),
        source.reshape(1, NREC),
        owner.reshape(1, NREC),
        slot.reshape(1, NREC),
        window.reshape(1, NREC),
        box.reshape(512, 128),
        speed.reshape(512, 128),
        jnp.asarray(tsyn), jnp.asarray(tana), jnp.asarray(grad), jnp.asarray(div),
    ]
    n_copies = 5 + 2 + ny - 1 + nz - 1
    hbm = pl.BlockSpec(memory_space=pltpu.HBM)
    vmem = pltpu.VMEM
    scratch = [vmem(a.shape, a.dtype) for a in args] + [
        vmem((RP, 1024), F32),
        vmem((RP, 1024), F32),
        vmem((RP, 128), F32),
        vmem((RP, 128), F32),
        vmem((512, 1024), BF16),
        vmem((192, 1024), BF16),
        vmem((512, 128), BF16),
        vmem((512, 128), BF16),
        vmem((256, 512), BF16),
        vmem((RP, 1024), F32),
        vmem((2, 8, 1024), F32),
        vmem((2, 8, 1024), F32),
        vmem((2, 16, 128), F32),
        vmem((64, 128), F32),
        vmem((2, 32, 128), F32),
        vmem((8, 128), F32),
        vmem((8, 128), F32),
        vmem((256, 256), BF16),
        vmem((256, 128), BF16),
        vmem((ny * nz * 8, 256), BF16),
        vmem((ny - 1, nz, 8, 128), BF16),
        vmem((nz, 8, 128), BF16),
        vmem((ny * nz, 8, 128), BF16),
        vmem((nz - 1, 8, 128), BF16),
        pltpu.SemaphoreType.DMA((15,)),
        pltpu.SemaphoreType.DMA((n_copies,)),
        pltpu.SemaphoreType.DMA((n_copies,)),
        pltpu.SemaphoreType.REGULAR((2,)),
    ]
    ga, ba = pl.pallas_call(
        functools.partial(kernel, ny, nz, nb),
        out_shape=(vmem((25, 2, 1024), F32), vmem((512, 128), F32)),
        in_specs=[hbm] * len(args),
        out_specs=(pl.BlockSpec(memory_space=vmem),) * 2,
        scratch_shapes=scratch,
        compiler_params=pltpu.CompilerParams(
            collective_id=0, has_side_effects=True, vmem_limit_bytes=40 * 2**20
        ),
        name="step",
    )(*[pltpu.with_memory_space_constraint(a, pltpu.HBM) for a in args])
    ga, ba = pl.pallas_call(
        write_out,
        out_shape=(jax.ShapeDtypeStruct((25, 2, 1024), F32), jax.ShapeDtypeStruct((512, 128), F32)),
        in_specs=[pl.BlockSpec(memory_space=vmem)] * 2,
        out_specs=(hbm, hbm),
        scratch_shapes=[pltpu.SemaphoreType.DMA((2,))],
        name="write_out",
    )(pltpu.with_memory_space_constraint(ga, vmem), pltpu.with_memory_space_constraint(ba, vmem))
    ga = ga.reshape(5, 5, 2, 1024).transpose(2, 0, 1, 3)
    return ga, ba.reshape(32, 16, 128)


def solution(mesh):
    n_mer = mesh.shape["mer"]
    nz = NZ_FULL if n_mer == 64 else 4
    d = P(("mer", "grp", "box"))
    return jax.shard_map(
        functools.partial(shards, n_mer // nz, nz, mesh.shape["box"]),
        mesh=mesh,
        in_specs=(d, d, d, d, d, d, d, d, d, P("mer", "box", "grp"), P("mer", "box", "grp")),
        out_specs=(d, P("mer", "box", "grp")),
        check_vma=False,
    )
```

```python
import functools
import math

import jax
import jax.numpy as jnp
import ml_dtypes
import numpy as np
from jax import lax
from jax.experimental import pallas as pl
from jax.experimental.pallas import tpu as pltpu
from jax.sharding import PartitionSpec as P

MESH = pl.DeviceIdType.MESH
F32 = jnp.float32
BF16 = jnp.bfloat16
NZ_FULL = 16
NREC = 128
RP = 64


def gll_derivative():
    nodes = np.array([-1.0, -math.sqrt(3.0 / 7.0), 0.0, math.sqrt(3.0 / 7.0), 1.0])
    legendre = (35.0 * nodes**4 - 30.0 * nodes**2 + 3.0) / 8.0
    table = np.zeros((5, 5))
    for i in range(5):
        for j in range(5):
            if i != j:
                table[i, j] = legendre[i] / (legendre[j] * (nodes[i] - nodes[j]))
    table[0, 0] = -5.0
    table[4, 4] = 5.0
    return table.astype(np.float32)


def split_bf16(matrix):
    hi = matrix.astype(ml_dtypes.bfloat16)
    lo = (matrix - hi.astype(np.float32)).astype(ml_dtypes.bfloat16)
    return hi, lo


def constants():
    order = np.arange(512)
    sample = np.arange(1024)
    angle = (order[:, None] * sample[None, :] % 1024) * (2.0 * math.pi / 1024)
    weight = np.where(order == 0, 1.0, 2.0)[:, None]
    synthesis = np.concatenate([weight * np.cos(angle), -weight * np.sin(angle)], 0)
    synthesis = synthesis.astype(np.float32).astype(ml_dtypes.bfloat16)
    deriv = gll_derivative()
    eye5, eye2 = np.eye(5, dtype=np.float32), np.eye(2, dtype=np.float32)
    d1 = np.zeros((RP, RP), np.float32)
    d2 = np.zeros((RP, RP), np.float32)
    d1[:50, :50] = np.kron(np.kron(deriv, eye5), eye2)
    d2[:50, :50] = np.kron(np.kron(eye5, deriv), eye2)
    h1, l1 = split_bf16(d1)
    h2, l2 = split_bf16(d2)
    grad = np.concatenate(
        [np.concatenate([h1, h1, l1], 1), np.concatenate([h2, h2, l2], 1)], 0
    )
    h1, l1, h2, l2 = h1.T, l1.T, h2.T, l2.T
    div = np.concatenate([h1, h2, h1, h2, l1, l2], 1)
    return synthesis[:, :512], grad, div


def dot(a, b):
    return jnp.dot(a, b, preferred_element_type=F32)


def kernel(
    ny, nz, nb,
    disp_h, rad_h, mod_h, imass_h, cnt_h, sp_h, ro_h, fs_h, ws_h, box_h, speed_h, tsyn_h, grad_h, div_h,
    ga, acc,
    disp, rad, mod, imass, cnt, sp, ro, fs, ws, box, speed, tsyn, gradm, divm,
    field, modf, radf, massf, lhs1, lhs2, pots, tracs, gather, divs,
    edge, edge_in, xin, yout, yin, zout, zin, spot, vals, route, part_in, line, face, face_in,
    in_sem, send_sem, recv_sem, relay_sem,
):
    mer = lax.axis_index("mer")
    grp = lax.axis_index("grp")
    bx = lax.axis_index("box")
    my_y = mer // nz
    my_z = mer % nz
    n_mer = ny * nz
    chain = (mer * 2 + grp) * nb + bx
    n_dev = n_mer * 2 * nb

    def chain_id(d):
        d = (d + n_dev) % n_dev
        return (d // (2 * nb), (d // nb) % 2, d % nb)

    mer_up = ((mer + 1) % n_mer, grp, bx)
    mer_down = ((mer + n_mer - 1) % n_mer, grp, bx)
    box_up = (mer, grp, (bx + 1) % nb)
    box_down = (mer, grp, (bx + nb - 1) % nb)
    other = (mer, 1 - grp, bx)
    next_id = chain_id(chain + 1)
    prev_id = chain_id(chain - 1)
    y_ahead = sorted(range(1, ny), key=lambda k: (-min(k, ny - k), k))
    z_ahead = sorted(range(1, nz), key=lambda k: (-min(k, nz - k), k))
    y_peers = [(((my_y + k) % ny) * nz + my_z, grp, bx) for k in y_ahead]
    z_peers = [(my_y * nz + (my_z + k) % nz, grp, bx) for k in z_ahead]
    reach = nz // 4
    relay_up = (my_y * nz + (my_z + reach) % nz, grp, bx)
    relay_down = (my_y * nz + (my_z + nz - reach) % nz, grp, bx)
    z_near = [z_peers[i] for i, k in enumerate(z_ahead) if min(k, nz - k) <= reach]
    partners = z_near + y_peers + [mer_up, mer_down, box_up, box_down, other, next_id, prev_id]

    barrier = pltpu.get_barrier_semaphore()
    for partner in partners:
        pl.semaphore_signal(barrier, inc=1, device_id=partner, device_id_type=MESH)

    loads = []
    for index, (src, dst) in enumerate(
        [
            (disp_h, disp), (cnt_h, cnt), (rad_h, rad), (grad_h, gradm), (tsyn_h, tsyn), (mod_h, mod), (sp_h, sp),
            (ws_h, ws), (ro_h, ro), (fs_h, fs), (box_h, box), (div_h, divm), (speed_h, speed),
            (imass_h, imass),
        ]
    ):
        copy = pltpu.make_async_copy(src, dst, in_sem.at[index])
        if index < 10:
            copy.start()
        loads.append(copy)
    (l_disp, l_cnt, l_rad, l_grad, l_tsyn, l_mod, l_sp, l_ws, l_ro, l_fs, l_box, l_div, l_speed, l_imass) = loads

    counter = [0]

    def remote(src, dst, partner):
        index = counter[0]
        counter[0] += 1
        copy = pltpu.make_async_remote_copy(
            src_ref=src, dst_ref=dst, send_sem=send_sem.at[index], recv_sem=recv_sem.at[index],
            device_id=partner, device_id_type=MESH,
        )
        copy.start()
        return copy

    lane = lax.broadcasted_iota(jnp.int32, (1, 1024), 1)
    order = lane & 511
    orderf = order.astype(F32)
    sign = (1 - 2 * (order & 1)).astype(BF16)
    row64 = lax.broadcasted_iota(jnp.int32, (RP, 1), 0)

    field[48:RP, :] = jnp.zeros((RP - 48, 1024), F32)
    radf[...] = jnp.ones((RP, 128), F32)
    l_disp.wait()
    for i in range(25):
        field[2 * i : 2 * i + 2, :] = disp[i]
    l_cnt.wait()
    counts = jnp.where((row64 & 1) == 0, cnt[0:1, 0:1], cnt[0:1, 1:2])
    mask = (order < counts).astype(F32)
    f = field[...] * mask
    l_rad.wait()
    for i in range(25):
        radf[2 * i : 2 * i + 2, :] = jnp.broadcast_to(rad[i // 5][:, i % 5 : i % 5 + 1], (2, 128))
    invr = (1.0 / radf[...])[:, 0:1]
    fhi = f.astype(BF16)
    flo = (f - fhi.astype(F32)).astype(BF16)
    l_grad.wait()
    g12 = dot(gradm[...], jnp.concatenate([fhi, flo, fhi], 0)).astype(BF16)
    lhs1[0:128, :] = g12
    lhs1[256:384, :] = g12 * sign
    g3 = (jnp.concatenate([-f[:, 512:], f[:, :512]], 1) * orderf * invr).astype(BF16)
    lhs1[128:192, :] = g3
    lhs1[384:448, :] = g3 * sign
    lhs1[192:256, :] = fhi
    lhs1[448:512, :] = fhi * sign

    l_sp.wait()
    l_ws.wait()
    second = (sp[...] >= 25).astype(jnp.int32)
    point = (sp[...] - 25 * second) * 2 + second
    packed = ((ws[...] >> 7) * RP + point) | ((ws[...] & 127) << 9)
    packed = jnp.broadcast_to(packed, (128, 128)).T
    key = packed & 511
    offset = packed >> 9
    lane128 = lax.broadcasted_iota(jnp.int32, (128, 128), 1)
    for t in range(4):
        cols = slice(t * 128, (t + 1) * 128)
        gather[0:128, cols] = (key == lane128 + t * 128).astype(F32).astype(BF16)
        gather[128:256, cols] = (key + RP == lane128 + t * 128).astype(F32).astype(BF16)

    l_ro.wait()
    l_fs.wait()
    row = lax.broadcasted_iota(jnp.int32, (ny * nz * 8, 128), 0)
    step = row >> 3
    target = (((my_y + step // nz) % ny) * nz + (my_z + step % nz) % nz) * 16 + (row & 7)
    keys = jnp.broadcast_to(ro[...] * 16 + fs[...], (ny * nz * 8, 128))
    route[:, 0:128] = (keys == target).astype(F32).astype(BF16)
    route[:, 128:256] = (keys == target + 8).astype(F32).astype(BF16)

    modf[48:RP, :] = jnp.zeros((RP - 48, 1024), F32)
    l_mod.wait()
    for i in range(25):
        modf[2 * i : 2 * i + 2, :] = mod[i].astype(F32)
    l_tsyn.wait()
    for copy in (l_box, l_div, l_speed, l_imass):
        copy.start()
    for s in range(2):
        half = slice(s * 512, (s + 1) * 512)
        phys = dot(lhs1[s * 256 : (s + 1) * 256, :], tsyn[...])
        for c in range(3):
            lhs2[s * 192 + c * RP : s * 192 + (c + 1) * RP, :] = (modf[:, half] * phys[c * RP : (c + 1) * RP]).astype(BF16)
        for t in range(4):
            b = s * 4 + t
            pots[b * RP : (b + 1) * RP, :] = phys[192:256, t * 128 : (t + 1) * 128].astype(BF16)

    coeffs = lax.dot_general(lhs2[...], tsyn[...], (((1,), (1,)), ((), ())), preferred_element_type=F32)
    scale = mask * jnp.where(order == 0, 1.0 / 1024, 1.0 / 2048)
    signed = scale * (1 - 2 * (order & 1)).astype(F32)
    c1, c2, c3 = (coeffs[c * RP : (c + 1) * RP] * scale + coeffs[192 + c * RP : 256 + c * RP] * signed for c in range(3))

    c2hi = c2.astype(BF16)
    synth = dot(jnp.concatenate([c2hi, c2hi * sign], 0), tsyn[...]).astype(BF16)
    for s in range(2):
        for t in range(4):
            b = s * 4 + t
            tracs[b * RP : (b + 1) * RP, :] = synth[s * RP : (s + 1) * RP, t * 128 : (t + 1) * 128]
    windows = []
    for table in (pots, tracs):
        got = dot(gather[...], table[...])
        windows.append(jnp.where(lane128 >= offset, got[0:128], got[128:256]))
    where = (offset + (lane128 & 31)) & 127
    pieces = [jnp.take_along_axis(window, where, axis=1, mode="promise_in_bounds") for window in windows]
    merged = jnp.where((lane128 & 32) == 0, pieces[0], pieces[1])
    vals[0:128, :] = jnp.where(lane128 < 64, merged, 0.0).astype(BF16)
    vals[128:256, :] = jnp.where(lane128 < 64, 0.0, merged).astype(BF16)
    face[...] = dot(route[...], vals[...]).reshape(ny * nz, 8, 128).astype(BF16)
    pl.semaphore_wait(barrier, len(partners))
    pl.semaphore_signal(relay_sem.at[0], inc=1, device_id=relay_up, device_id_type=MESH)
    pl.semaphore_signal(relay_sem.at[1], inc=1, device_id=relay_down, device_id_type=MESH)
    part_copies = [
        remote(face.at[pl.ds(step * nz, nz)], part_in.at[k], y_peers[k]) for k, step in enumerate(y_ahead)
    ]
    l_box.wait()
    yout[0:32, :] = box[pl.ds(0, 32, stride=16), :]
    yout[32:64, :] = box[pl.ds(15, 32, stride=16), :]
    far_lane = 127 * (1 - grp)
    near_lane = 127 * grp
    row128 = lax.broadcasted_iota(jnp.int32, (128, 128), 0)
    pick = (row128 == far_lane).astype(F32).astype(BF16)
    column = dot(box[...].astype(BF16), pick).reshape(64, 8, 128)
    block64 = lax.broadcasted_iota(jnp.int32, (64, 1, 128), 0)
    lane64 = lax.broadcasted_iota(jnp.int32, (64, 1, 128), 2)
    place = (block64 >> 1) + (block64 & 1) * 64
    pot_mask = lane64 == place
    trac_mask = lane64 == place + 32
    zout[...] = jnp.sum(jnp.where(pot_mask, column, 0.0), axis=0)
    x_copies = [
        remote(box.at[pl.ds(0, 16)], xin.at[1], mer_down),
        remote(box.at[pl.ds(496, 16)], xin.at[0], mer_up),
    ]
    y_copies = [
        remote(yout.at[pl.ds(0, 32)], yin.at[1], box_down),
        remote(yout.at[pl.ds(32, 32)], yin.at[0], box_up),
    ]
    z_copy = remote(zout, zin, other)

    c1hi = c1.astype(BF16)
    c1lo = (c1 - c1hi.astype(F32)).astype(BF16)
    c2lo = (c2 - c2hi.astype(F32)).astype(BF16)
    l_div.wait()
    div = dot(divm[...], jnp.concatenate([c1hi, c2hi, c1lo, c2lo, c1hi, c2hi], 0))
    div = div + jnp.concatenate([c3[:, 512:], -c3[:, :512]], 1) * orderf * invr
    divs[...] = div
    for k in range(5):
        edge[0, k : k + 1, :] = divs[41 + 2 * k : 42 + 2 * k, :]
        edge[1, k : k + 1, :] = divs[2 * k : 2 * k + 1, :]
    edge[0, 5:8, :] = jnp.zeros((3, 1024), F32)
    edge[1, 5:8, :] = jnp.zeros((3, 1024), F32)
    edge_copies = [
        remote(edge.at[0], edge_in.at[0], next_id),
        remote(edge.at[1], edge_in.at[1], prev_id),
    ]

    l_speed.wait()
    b = box[...]
    row512 = lax.broadcasted_iota(jnp.int32, (512, 128), 0) & 15
    lane512 = lax.broadcasted_iota(jnp.int32, (512, 128), 1)
    zero16 = jnp.zeros((16, 128), F32)
    total = jnp.concatenate([zero16, b[:-16]], 0) + jnp.concatenate([b[16:], zero16], 0)
    total = total + jnp.where(row512 == 0, 0.0, pltpu.roll(b, 1, 0)) + jnp.where(row512 == 15, 0.0, pltpu.roll(b, 511, 0))
    total = total + jnp.where(lane512 == 0, 0.0, pltpu.roll(b, 1, 1)) + jnp.where(lane512 == 127, 0.0, pltpu.roll(b, 127, 1))
    acc[...] = speed[...] * (total - 6.0 * b)

    part = face[0:nz].astype(F32)
    for k, copy in enumerate(part_copies):
        copy.wait_recv()
        part = part + part_in[k].astype(F32)
    line[...] = part.astype(BF16)
    pl.semaphore_wait(relay_sem.at[0], 1)
    pl.semaphore_wait(relay_sem.at[1], 1)
    face_copies = [remote(line.at[step], face_in.at[k], z_peers[k]) for k, step in enumerate(z_ahead)]

    for copy in x_copies + y_copies + [z_copy]:
        copy.wait_recv()
    acc[0:16, :] += speed[0:16, :] * jnp.where(mer == 0, 0.0, xin[0])
    acc[496:512, :] += speed[496:512, :] * jnp.where(mer == n_mer - 1, 0.0, xin[1])
    acc[pl.ds(0, 32, stride=16), :] += speed[pl.ds(0, 32, stride=16), :] * jnp.where(bx == 0, 0.0, yin[0])
    acc[pl.ds(15, 32, stride=16), :] += speed[pl.ds(15, 32, stride=16), :] * jnp.where(bx == nb - 1, 0.0, yin[1])
    lane128 = lax.broadcasted_iota(jnp.int32, (128, 128), 1)
    far = (lane128 == far_lane).astype(F32).astype(BF16)
    spread = jnp.where(pot_mask, zin[...][None], 0.0).reshape(512, 128)
    acc[...] += speed[...] * dot(spread.astype(BF16), far)

    l_imass.wait()
    for i in range(25):
        massf[2 * i : 2 * i + 2, :] = jnp.broadcast_to(imass[i // 5][:, i % 5 : i % 5 + 1], (2, 128))
    for copy in edge_copies:
        copy.wait_recv()
    for k in range(5):
        inner = divs[40 + 2 * k : 41 + 2 * k, :] + divs[1 + 2 * k : 2 + 2 * k, :]
        divs[40 + 2 * k : 41 + 2 * k, :] = inner
        divs[1 + 2 * k : 2 + 2 * k, :] = inner
        divs[2 * k : 2 * k + 1, :] += jnp.where(chain == 0, 0.0, edge_in[0, k : k + 1, :])
        divs[41 + 2 * k : 42 + 2 * k, :] += jnp.where(chain == n_dev - 1, 0.0, edge_in[1, k : k + 1, :])
    for i in range(25):
        ga[i] = divs[2 * i : 2 * i + 2, :] * -massf[2 * i : 2 * i + 2, 0:1]

    both_mask = pot_mask | trac_mask
    row256 = lax.broadcasted_iota(jnp.int32, (256, 256), 0)
    col256 = lax.broadcasted_iota(jnp.int32, (256, 256), 1)
    keep = ((row256 & 32) == 0) == (col256 < 128)
    spot[...] = (keep & ((col256 & 127) == near_lane)).astype(F32).astype(BF16)
    for copy in x_copies + y_copies + [z_copy] + part_copies + edge_copies + face_copies:
        copy.wait_send()
    cut = len(face_copies) // 2
    mine = part[0]
    for first, last in ((cut, len(face_copies)), (0, cut)):
        if first < last:
            for k in range(last - 1, first - 1, -1):
                face_copies[k].wait_recv()
            mine = mine + jnp.sum(face_in[first:last].astype(F32), axis=0)
    hi = mine.astype(BF16).astype(F32)
    lo = mine - hi
    hi = jnp.where(both_mask, hi[None], 0.0).reshape(512, 128).astype(BF16)
    lo = jnp.where(both_mask, lo[None], 0.0).reshape(512, 128).astype(BF16)
    sides = dot(jnp.concatenate([hi, lo], 1), spot[...])
    acc[...] += speed[...] * sides[:, :128] + 0.25 * sides[:, 128:]


def write_out(ga, ba, ga_h, ba_h, sem):
    copies = [pltpu.make_async_copy(ga, ga_h, sem.at[0]), pltpu.make_async_copy(ba, ba_h, sem.at[1])]
    for copy in copies:
        copy.start()
    for copy in copies:
        copy.wait()


def shards(ny, nz, nb, displacement, radius, bulk, imass, counts, source, owner, slot, window, box, speed):
    tsyn, grad, div = constants()
    args = [
        displacement.transpose(1, 2, 0, 3).reshape(25, 2, 1024),
        radius.transpose(1, 0, 2),
        bulk.transpose(1, 2, 0, 3).reshape(25, 2, 1024),
        imass.transpose(1, 0, 2),
        counts.reshape(1, 2),
        source.reshape(1, NREC),
        owner.reshape(1, NREC),
        slot.reshape(1, NREC),
        window.reshape(1, NREC),
        box.reshape(512, 128),
        speed.reshape(512, 128),
        jnp.asarray(tsyn), jnp.asarray(grad), jnp.asarray(div),
    ]
    n_copies = 5 + 2 + ny - 1 + nz - 1
    hbm = pl.BlockSpec(memory_space=pltpu.HBM)
    vmem = pltpu.VMEM
    scratch = [vmem(a.shape, a.dtype) for a in args] + [
        vmem((RP, 1024), F32),
        vmem((RP, 1024), F32),
        vmem((RP, 128), F32),
        vmem((RP, 128), F32),
        vmem((512, 1024), BF16),
        vmem((384, 512), BF16),
        vmem((512, 128), BF16),
        vmem((512, 128), BF16),
        vmem((256, 512), BF16),
        vmem((RP, 1024), F32),
        vmem((2, 8, 1024), F32),
        vmem((2, 8, 1024), F32),
        vmem((2, 16, 128), F32),
        vmem((64, 128), F32),
        vmem((2, 32, 128), F32),
        vmem((8, 128), F32),
        vmem((8, 128), F32),
        vmem((256, 256), BF16),
        vmem((256, 128), BF16),
        vmem((ny * nz * 8, 256), BF16),
        vmem((ny - 1, nz, 8, 128), BF16),
        vmem((nz, 8, 128), BF16),
        vmem((ny * nz, 8, 128), BF16),
        vmem((nz - 1, 8, 128), BF16),
        pltpu.SemaphoreType.DMA((14,)),
        pltpu.SemaphoreType.DMA((n_copies,)),
        pltpu.SemaphoreType.DMA((n_copies,)),
        pltpu.SemaphoreType.REGULAR((2,)),
    ]
    ga, ba = pl.pallas_call(
        functools.partial(kernel, ny, nz, nb),
        out_shape=(vmem((25, 2, 1024), F32), vmem((512, 128), F32)),
        in_specs=[hbm] * len(args),
        out_specs=(pl.BlockSpec(memory_space=vmem),) * 2,
        scratch_shapes=scratch,
        compiler_params=pltpu.CompilerParams(
            collective_id=0, has_side_effects=True, vmem_limit_bytes=40 * 2**20
        ),
        name="step",
    )(*[pltpu.with_memory_space_constraint(a, pltpu.HBM) for a in args])
    ga, ba = pl.pallas_call(
        write_out,
        out_shape=(jax.ShapeDtypeStruct((25, 2, 1024), F32), jax.ShapeDtypeStruct((512, 128), F32)),
        in_specs=[pl.BlockSpec(memory_space=vmem)] * 2,
        out_specs=(hbm, hbm),
        scratch_shapes=[pltpu.SemaphoreType.DMA((2,))],
        name="write_out",
    )(pltpu.with_memory_space_constraint(ga, vmem), pltpu.with_memory_space_constraint(ba, vmem))
    ga = ga.reshape(5, 5, 2, 1024).transpose(2, 0, 1, 3)
    return ga, ba.reshape(32, 16, 128)


def solution(mesh):
    n_mer = mesh.shape["mer"]
    nz = NZ_FULL if n_mer == 64 else 4
    d = P(("mer", "grp", "box"))
    return jax.shard_map(
        functools.partial(shards, n_mer // nz, nz, mesh.shape["box"]),
        mesh=mesh,
        in_specs=(d, d, d, d, d, d, d, d, d, P("mer", "box", "grp"), P("mer", "box", "grp")),
        out_specs=(d, P("mer", "box", "grp")),
        check_vma=False,
    )
```

```python
import functools
import math

import jax
import jax.numpy as jnp
import ml_dtypes
import numpy as np
from jax import lax
from jax.experimental import pallas as pl
from jax.experimental.pallas import tpu as pltpu
from jax.sharding import PartitionSpec as P

MESH = pl.DeviceIdType.MESH
F32 = jnp.float32
BF16 = jnp.bfloat16
NZ_FULL = 16
NREC = 128
RP = 64


def gll_derivative():
    nodes = np.array([-1.0, -math.sqrt(3.0 / 7.0), 0.0, math.sqrt(3.0 / 7.0), 1.0])
    legendre = (35.0 * nodes**4 - 30.0 * nodes**2 + 3.0) / 8.0
    table = np.zeros((5, 5))
    for i in range(5):
        for j in range(5):
            if i != j:
                table[i, j] = legendre[i] / (legendre[j] * (nodes[i] - nodes[j]))
    table[0, 0] = -5.0
    table[4, 4] = 5.0
    return table.astype(np.float32)


def split_bf16(matrix):
    hi = matrix.astype(ml_dtypes.bfloat16)
    lo = (matrix - hi.astype(np.float32)).astype(ml_dtypes.bfloat16)
    return hi, lo


def constants():
    order = np.arange(512)
    sample = np.arange(1024)
    angle = (order[:, None] * sample[None, :] % 1024) * (2.0 * math.pi / 1024)
    weight = np.where(order == 0, 1.0, 2.0)[:, None]
    synthesis = np.concatenate([weight * np.cos(angle), -weight * np.sin(angle)], 0)
    synthesis = synthesis.astype(np.float32).astype(ml_dtypes.bfloat16)
    deriv = gll_derivative()
    eye5, eye2 = np.eye(5, dtype=np.float32), np.eye(2, dtype=np.float32)
    d1 = np.zeros((RP, RP), np.float32)
    d2 = np.zeros((RP, RP), np.float32)
    d1[:50, :50] = np.kron(np.kron(deriv, eye5), eye2)
    d2[:50, :50] = np.kron(np.kron(eye5, deriv), eye2)
    h1, l1 = split_bf16(d1)
    h2, l2 = split_bf16(d2)
    grad = np.concatenate(
        [np.concatenate([h1, h1, l1], 1), np.concatenate([h2, h2, l2], 1)], 0
    )
    h1, l1, h2, l2 = h1.T, l1.T, h2.T, l2.T
    div = np.concatenate([h1, h2, h1, h2, l1, l2], 1)
    return synthesis[:, :512], grad, div


def dot(a, b):
    return jnp.dot(a, b, preferred_element_type=F32)


def kernel(
    ny, nz, nb,
    disp_h, rad_h, mod_h, imass_h, cnt_h, sp_h, ro_h, fs_h, ws_h, box_h, speed_h, tsyn_h, grad_h, div_h,
    ga, acc,
    disp, rad, mod, imass, cnt, sp, ro, fs, ws, box, speed, tsyn, gradm, divm,
    field, modf, radf, massf, lhs1, lhs2, pots, tracs, gather, divs,
    edge, edge_in, xin, yout, yin, zout, zin, spot, vals, route, part_in, line, face, face_in,
    in_sem, send_sem, recv_sem, relay_sem,
):
    mer = lax.axis_index("mer")
    grp = lax.axis_index("grp")
    bx = lax.axis_index("box")
    my_y = mer // nz
    my_z = mer % nz
    n_mer = ny * nz
    chain = (mer * 2 + grp) * nb + bx
    n_dev = n_mer * 2 * nb

    def chain_id(d):
        d = (d + n_dev) % n_dev
        return (d // (2 * nb), (d // nb) % 2, d % nb)

    mer_up = ((mer + 1) % n_mer, grp, bx)
    mer_down = ((mer + n_mer - 1) % n_mer, grp, bx)
    box_up = (mer, grp, (bx + 1) % nb)
    box_down = (mer, grp, (bx + nb - 1) % nb)
    other = (mer, 1 - grp, bx)
    next_id = chain_id(chain + 1)
    prev_id = chain_id(chain - 1)
    y_ahead = sorted(range(1, ny), key=lambda k: (-min(k, ny - k), k))
    z_ahead = sorted(range(1, nz), key=lambda k: (-min(k, nz - k), k))
    y_peers = [(((my_y + k) % ny) * nz + my_z, grp, bx) for k in y_ahead]
    z_peers = [(my_y * nz + (my_z + k) % nz, grp, bx) for k in z_ahead]
    reach = nz // 4
    relay_up = (my_y * nz + (my_z + reach) % nz, grp, bx)
    relay_down = (my_y * nz + (my_z + nz - reach) % nz, grp, bx)
    z_near = [z_peers[i] for i, k in enumerate(z_ahead) if min(k, nz - k) <= reach]
    partners = z_near + y_peers + [mer_up, mer_down, box_up, box_down, other, next_id, prev_id]

    barrier = pltpu.get_barrier_semaphore()
    for partner in partners:
        pl.semaphore_signal(barrier, inc=1, device_id=partner, device_id_type=MESH)

    loads = []
    for index, (src, dst) in enumerate(
        [
            (disp_h, disp), (cnt_h, cnt), (rad_h, rad), (grad_h, gradm), (tsyn_h, tsyn), (mod_h, mod), (sp_h, sp),
            (ws_h, ws), (ro_h, ro), (fs_h, fs), (box_h, box), (div_h, divm), (speed_h, speed),
            (imass_h, imass),
        ]
    ):
        copy = pltpu.make_async_copy(src, dst, in_sem.at[index])
        if index < 10:
            copy.start()
        loads.append(copy)
    (l_disp, l_cnt, l_rad, l_grad, l_tsyn, l_mod, l_sp, l_ws, l_ro, l_fs, l_box, l_div, l_speed, l_imass) = loads

    counter = [0]

    def remote(src, dst, partner):
        index = counter[0]
        counter[0] += 1
        copy = pltpu.make_async_remote_copy(
            src_ref=src, dst_ref=dst, send_sem=send_sem.at[index], recv_sem=recv_sem.at[index],
            device_id=partner, device_id_type=MESH,
        )
        copy.start()
        return copy

    lane = lax.broadcasted_iota(jnp.int32, (1, 1024), 1)
    order = lane & 511
    orderf = order.astype(F32)
    sign = (1 - 2 * (order & 1)).astype(BF16)
    row64 = lax.broadcasted_iota(jnp.int32, (RP, 1), 0)

    field[48:RP, :] = jnp.zeros((RP - 48, 1024), F32)
    radf[...] = jnp.ones((RP, 128), F32)
    l_disp.wait()
    for i in range(25):
        field[2 * i : 2 * i + 2, :] = disp[i]
    l_cnt.wait()
    counts = jnp.where((row64 & 1) == 0, cnt[0:1, 0:1], cnt[0:1, 1:2])
    mask = (order < counts).astype(F32)
    f = field[...] * mask
    l_rad.wait()
    for i in range(25):
        radf[2 * i : 2 * i + 2, :] = jnp.broadcast_to(rad[i // 5][:, i % 5 : i % 5 + 1], (2, 128))
    invr = (1.0 / radf[...])[:, 0:1]
    fhi = f.astype(BF16)
    flo = (f - fhi.astype(F32)).astype(BF16)
    l_grad.wait()
    g12 = dot(gradm[...], jnp.concatenate([fhi, flo, fhi], 0)).astype(BF16)
    lhs1[0:128, :] = g12
    lhs1[256:384, :] = g12 * sign
    g3 = (jnp.concatenate([-f[:, 512:], f[:, :512]], 1) * orderf * invr).astype(BF16)
    lhs1[128:192, :] = g3
    lhs1[384:448, :] = g3 * sign
    lhs1[192:256, :] = fhi
    lhs1[448:512, :] = fhi * sign

    l_sp.wait()
    l_ws.wait()
    second = (sp[...] >= 25).astype(jnp.int32)
    point = (sp[...] - 25 * second) * 2 + second
    packed = ((ws[...] >> 7) * RP + point) | ((ws[...] & 127) << 9)
    packed = jnp.broadcast_to(packed, (128, 128)).T
    key = packed & 511
    offset = packed >> 9
    lane128 = lax.broadcasted_iota(jnp.int32, (128, 128), 1)
    for t in range(4):
        cols = slice(t * 128, (t + 1) * 128)
        gather[0:128, cols] = (key == lane128 + t * 128).astype(F32).astype(BF16)
        gather[128:256, cols] = (key + RP == lane128 + t * 128).astype(F32).astype(BF16)

    l_ro.wait()
    l_fs.wait()
    row = lax.broadcasted_iota(jnp.int32, (ny * nz * 8, 128), 0)
    step = row >> 3
    target = (((my_y + step // nz) % ny) * nz + (my_z + step % nz) % nz) * 16 + (row & 7)
    keys = jnp.broadcast_to(ro[...] * 16 + fs[...], (ny * nz * 8, 128))
    route[:, 0:128] = (keys == target).astype(F32).astype(BF16)
    route[:, 128:256] = (keys == target + 8).astype(F32).astype(BF16)

    modf[48:RP, :] = jnp.zeros((RP - 48, 1024), F32)
    l_mod.wait()
    for i in range(25):
        modf[2 * i : 2 * i + 2, :] = mod[i].astype(F32)
    l_tsyn.wait()
    for copy in (l_box, l_div, l_speed, l_imass):
        copy.start()
    for s in range(2):
        half = slice(s * 512, (s + 1) * 512)
        phys = dot(lhs1[s * 256 : (s + 1) * 256, :], tsyn[...])
        for c in range(3):
            lhs2[s * 192 + c * RP : s * 192 + (c + 1) * RP, :] = (modf[:, half] * phys[c * RP : (c + 1) * RP]).astype(BF16)
        for t in range(4):
            b = s * 4 + t
            pots[b * RP : (b + 1) * RP, :] = phys[192:256, t * 128 : (t + 1) * 128].astype(BF16)

    scale = mask * jnp.where(order == 0, 1.0 / 1024, 1.0 / 2048)
    signed = scale * (1 - 2 * (order & 1)).astype(F32)

    def analyse(c):
        rows = jnp.concatenate([lhs2[c * RP : (c + 1) * RP, :], lhs2[192 + c * RP : 256 + c * RP, :]], 0)
        sums = lax.dot_general(rows, tsyn[...], (((1,), (1,)), ((), ())), preferred_element_type=F32)
        return sums[:RP] * scale + sums[RP:] * signed

    c2 = analyse(1)

    c2hi = c2.astype(BF16)
    synth = dot(jnp.concatenate([c2hi, c2hi * sign], 0), tsyn[...]).astype(BF16)
    for s in range(2):
        for t in range(4):
            b = s * 4 + t
            tracs[b * RP : (b + 1) * RP, :] = synth[s * RP : (s + 1) * RP, t * 128 : (t + 1) * 128]
    windows = []
    for table in (pots, tracs):
        got = dot(gather[...], table[...])
        windows.append(jnp.where(lane128 >= offset, got[0:128], got[128:256]))
    where = (offset + (lane128 & 31)) & 127
    pieces = [jnp.take_along_axis(window, where, axis=1, mode="promise_in_bounds") for window in windows]
    merged = jnp.where((lane128 & 32) == 0, pieces[0], pieces[1])
    vals[0:128, :] = jnp.where(lane128 < 64, merged, 0.0).astype(BF16)
    vals[128:256, :] = jnp.where(lane128 < 64, 0.0, merged).astype(BF16)
    face[...] = dot(route[...], vals[...]).reshape(ny * nz, 8, 128).astype(BF16)
    pl.semaphore_wait(barrier, len(partners))
    pl.semaphore_signal(relay_sem.at[0], inc=1, device_id=relay_up, device_id_type=MESH)
    pl.semaphore_signal(relay_sem.at[1], inc=1, device_id=relay_down, device_id_type=MESH)
    part_copies = [
        remote(face.at[pl.ds(step * nz, nz)], part_in.at[k], y_peers[k]) for k, step in enumerate(y_ahead)
    ]
    l_box.wait()
    yout[0:32, :] = box[pl.ds(0, 32, stride=16), :]
    yout[32:64, :] = box[pl.ds(15, 32, stride=16), :]
    far_lane = 127 * (1 - grp)
    near_lane = 127 * grp
    row128 = lax.broadcasted_iota(jnp.int32, (128, 128), 0)
    pick = (row128 == far_lane).astype(F32).astype(BF16)
    column = dot(box[...].astype(BF16), pick).reshape(64, 8, 128)
    block64 = lax.broadcasted_iota(jnp.int32, (64, 1, 128), 0)
    lane64 = lax.broadcasted_iota(jnp.int32, (64, 1, 128), 2)
    place = (block64 >> 1) + (block64 & 1) * 64
    pot_mask = lane64 == place
    trac_mask = lane64 == place + 32
    zout[...] = jnp.sum(jnp.where(pot_mask, column, 0.0), axis=0)
    x_copies = [
        remote(box.at[pl.ds(0, 16)], xin.at[1], mer_down),
        remote(box.at[pl.ds(496, 16)], xin.at[0], mer_up),
    ]
    y_copies = [
        remote(yout.at[pl.ds(0, 32)], yin.at[1], box_down),
        remote(yout.at[pl.ds(32, 32)], yin.at[0], box_up),
    ]
    z_copy = remote(zout, zin, other)

    c1, c3 = analyse(0), analyse(2)
    c1hi = c1.astype(BF16)
    c1lo = (c1 - c1hi.astype(F32)).astype(BF16)
    c2lo = (c2 - c2hi.astype(F32)).astype(BF16)
    l_div.wait()
    div = dot(divm[...], jnp.concatenate([c1hi, c2hi, c1lo, c2lo, c1hi, c2hi], 0))
    div = div + jnp.concatenate([c3[:, 512:], -c3[:, :512]], 1) * orderf * invr
    divs[...] = div
    for k in range(5):
        edge[0, k : k + 1, :] = divs[41 + 2 * k : 42 + 2 * k, :]
        edge[1, k : k + 1, :] = divs[2 * k : 2 * k + 1, :]
    edge[0, 5:8, :] = jnp.zeros((3, 1024), F32)
    edge[1, 5:8, :] = jnp.zeros((3, 1024), F32)
    edge_copies = [
        remote(edge.at[0], edge_in.at[0], next_id),
        remote(edge.at[1], edge_in.at[1], prev_id),
    ]

    l_speed.wait()
    b = box[...]
    row512 = lax.broadcasted_iota(jnp.int32, (512, 128), 0) & 15
    lane512 = lax.broadcasted_iota(jnp.int32, (512, 128), 1)
    zero16 = jnp.zeros((16, 128), F32)
    total = jnp.concatenate([zero16, b[:-16]], 0) + jnp.concatenate([b[16:], zero16], 0)
    total = total + jnp.where(row512 == 0, 0.0, pltpu.roll(b, 1, 0)) + jnp.where(row512 == 15, 0.0, pltpu.roll(b, 511, 0))
    total = total + jnp.where(lane512 == 0, 0.0, pltpu.roll(b, 1, 1)) + jnp.where(lane512 == 127, 0.0, pltpu.roll(b, 127, 1))
    acc[...] = speed[...] * (total - 6.0 * b)

    part = face[0:nz].astype(F32)
    for k, copy in enumerate(part_copies):
        copy.wait_recv()
        part = part + part_in[k].astype(F32)
    line[...] = part.astype(BF16)
    pl.semaphore_wait(relay_sem.at[0], 1)
    pl.semaphore_wait(relay_sem.at[1], 1)
    face_copies = [remote(line.at[step], face_in.at[k], z_peers[k]) for k, step in enumerate(z_ahead)]

    for copy in x_copies + y_copies + [z_copy]:
        copy.wait_recv()
    acc[0:16, :] += speed[0:16, :] * jnp.where(mer == 0, 0.0, xin[0])
    acc[496:512, :] += speed[496:512, :] * jnp.where(mer == n_mer - 1, 0.0, xin[1])
    acc[pl.ds(0, 32, stride=16), :] += speed[pl.ds(0, 32, stride=16), :] * jnp.where(bx == 0, 0.0, yin[0])
    acc[pl.ds(15, 32, stride=16), :] += speed[pl.ds(15, 32, stride=16), :] * jnp.where(bx == nb - 1, 0.0, yin[1])
    lane128 = lax.broadcasted_iota(jnp.int32, (128, 128), 1)
    far = (lane128 == far_lane).astype(F32).astype(BF16)
    spread = jnp.where(pot_mask, zin[...][None], 0.0).reshape(512, 128)
    acc[...] += speed[...] * dot(spread.astype(BF16), far)

    l_imass.wait()
    for i in range(25):
        massf[2 * i : 2 * i + 2, :] = jnp.broadcast_to(imass[i // 5][:, i % 5 : i % 5 + 1], (2, 128))
    for copy in edge_copies:
        copy.wait_recv()
    for k in range(5):
        inner = divs[40 + 2 * k : 41 + 2 * k, :] + divs[1 + 2 * k : 2 + 2 * k, :]
        divs[40 + 2 * k : 41 + 2 * k, :] = inner
        divs[1 + 2 * k : 2 + 2 * k, :] = inner
        divs[2 * k : 2 * k + 1, :] += jnp.where(chain == 0, 0.0, edge_in[0, k : k + 1, :])
        divs[41 + 2 * k : 42 + 2 * k, :] += jnp.where(chain == n_dev - 1, 0.0, edge_in[1, k : k + 1, :])
    for i in range(25):
        ga[i] = divs[2 * i : 2 * i + 2, :] * -massf[2 * i : 2 * i + 2, 0:1]

    both_mask = pot_mask | trac_mask
    row256 = lax.broadcasted_iota(jnp.int32, (256, 256), 0)
    col256 = lax.broadcasted_iota(jnp.int32, (256, 256), 1)
    keep = ((row256 & 32) == 0) == (col256 < 128)
    spot[...] = (keep & ((col256 & 127) == near_lane)).astype(F32).astype(BF16)
    for copy in x_copies + y_copies + [z_copy] + part_copies + edge_copies + face_copies:
        copy.wait_send()
    cut = len(face_copies) // 2
    mine = part[0]
    for first, last in ((cut, len(face_copies)), (0, cut)):
        if first < last:
            for k in range(last - 1, first - 1, -1):
                face_copies[k].wait_recv()
            mine = mine + jnp.sum(face_in[first:last].astype(F32), axis=0)
    hi = mine.astype(BF16).astype(F32)
    lo = mine - hi
    hi = jnp.where(both_mask, hi[None], 0.0).reshape(512, 128).astype(BF16)
    lo = jnp.where(both_mask, lo[None], 0.0).reshape(512, 128).astype(BF16)
    sides = dot(jnp.concatenate([hi, lo], 1), spot[...])
    acc[...] += speed[...] * sides[:, :128] + 0.25 * sides[:, 128:]


def write_out(ga, ba, ga_h, ba_h, sem):
    copies = [pltpu.make_async_copy(ga, ga_h, sem.at[0]), pltpu.make_async_copy(ba, ba_h, sem.at[1])]
    for copy in copies:
        copy.start()
    for copy in copies:
        copy.wait()


def shards(ny, nz, nb, displacement, radius, bulk, imass, counts, source, owner, slot, window, box, speed):
    tsyn, grad, div = constants()
    args = [
        displacement.transpose(1, 2, 0, 3).reshape(25, 2, 1024),
        radius.transpose(1, 0, 2),
        bulk.transpose(1, 2, 0, 3).reshape(25, 2, 1024),
        imass.transpose(1, 0, 2),
        counts.reshape(1, 2),
        source.reshape(1, NREC),
        owner.reshape(1, NREC),
        slot.reshape(1, NREC),
        window.reshape(1, NREC),
        box.reshape(512, 128),
        speed.reshape(512, 128),
        jnp.asarray(tsyn), jnp.asarray(grad), jnp.asarray(div),
    ]
    n_copies = 5 + 2 + ny - 1 + nz - 1
    hbm = pl.BlockSpec(memory_space=pltpu.HBM)
    vmem = pltpu.VMEM
    scratch = [vmem(a.shape, a.dtype) for a in args] + [
        vmem((RP, 1024), F32),
        vmem((RP, 1024), F32),
        vmem((RP, 128), F32),
        vmem((RP, 128), F32),
        vmem((512, 1024), BF16),
        vmem((384, 512), BF16),
        vmem((512, 128), BF16),
        vmem((512, 128), BF16),
        vmem((256, 512), BF16),
        vmem((RP, 1024), F32),
        vmem((2, 8, 1024), F32),
        vmem((2, 8, 1024), F32),
        vmem((2, 16, 128), F32),
        vmem((64, 128), F32),
        vmem((2, 32, 128), F32),
        vmem((8, 128), F32),
        vmem((8, 128), F32),
        vmem((256, 256), BF16),
        vmem((256, 128), BF16),
        vmem((ny * nz * 8, 256), BF16),
        vmem((ny - 1, nz, 8, 128), BF16),
        vmem((nz, 8, 128), BF16),
        vmem((ny * nz, 8, 128), BF16),
        vmem((nz - 1, 8, 128), BF16),
        pltpu.SemaphoreType.DMA((14,)),
        pltpu.SemaphoreType.DMA((n_copies,)),
        pltpu.SemaphoreType.DMA((n_copies,)),
        pltpu.SemaphoreType.REGULAR((2,)),
    ]
    ga, ba = pl.pallas_call(
        functools.partial(kernel, ny, nz, nb),
        out_shape=(vmem((25, 2, 1024), F32), vmem((512, 128), F32)),
        in_specs=[hbm] * len(args),
        out_specs=(pl.BlockSpec(memory_space=vmem),) * 2,
        scratch_shapes=scratch,
        compiler_params=pltpu.CompilerParams(
            collective_id=0, has_side_effects=True, vmem_limit_bytes=40 * 2**20
        ),
        name="step",
    )(*[pltpu.with_memory_space_constraint(a, pltpu.HBM) for a in args])
    ga, ba = pl.pallas_call(
        write_out,
        out_shape=(jax.ShapeDtypeStruct((25, 2, 1024), F32), jax.ShapeDtypeStruct((512, 128), F32)),
        in_specs=[pl.BlockSpec(memory_space=vmem)] * 2,
        out_specs=(hbm, hbm),
        scratch_shapes=[pltpu.SemaphoreType.DMA((2,))],
        name="write_out",
    )(pltpu.with_memory_space_constraint(ga, vmem), pltpu.with_memory_space_constraint(ba, vmem))
    ga = ga.reshape(5, 5, 2, 1024).transpose(2, 0, 1, 3)
    return ga, ba.reshape(32, 16, 128)


def solution(mesh):
    n_mer = mesh.shape["mer"]
    nz = NZ_FULL if n_mer == 64 else 4
    d = P(("mer", "grp", "box"))
    return jax.shard_map(
        functools.partial(shards, n_mer // nz, nz, mesh.shape["box"]),
        mesh=mesh,
        in_specs=(d, d, d, d, d, d, d, d, d, P("mer", "box", "grp"), P("mer", "box", "grp")),
        out_specs=(d, P("mer", "box", "grp")),
        check_vma=False,
    )
```

```python
import functools
import math

import jax
import jax.numpy as jnp
import ml_dtypes
import numpy as np
from jax import lax
from jax.experimental import pallas as pl
from jax.experimental.pallas import tpu as pltpu
from jax.sharding import PartitionSpec as P

MESH = pl.DeviceIdType.MESH
F32 = jnp.float32
BF16 = jnp.bfloat16
NZ_FULL = 16
NREC = 128
RP = 64


def gll_derivative():
    nodes = np.array([-1.0, -math.sqrt(3.0 / 7.0), 0.0, math.sqrt(3.0 / 7.0), 1.0])
    legendre = (35.0 * nodes**4 - 30.0 * nodes**2 + 3.0) / 8.0
    table = np.zeros((5, 5))
    for i in range(5):
        for j in range(5):
            if i != j:
                table[i, j] = legendre[i] / (legendre[j] * (nodes[i] - nodes[j]))
    table[0, 0] = -5.0
    table[4, 4] = 5.0
    return table.astype(np.float32)


def split_bf16(matrix):
    hi = matrix.astype(ml_dtypes.bfloat16)
    lo = (matrix - hi.astype(np.float32)).astype(ml_dtypes.bfloat16)
    return hi, lo


def constants():
    order = np.arange(512)
    sample = np.arange(1024)
    angle = (order[:, None] * sample[None, :] % 1024) * (2.0 * math.pi / 1024)
    weight = np.where(order == 0, 1.0, 2.0)[:, None]
    synthesis = np.concatenate([weight * np.cos(angle), -weight * np.sin(angle)], 0)
    synthesis = synthesis.astype(np.float32).astype(ml_dtypes.bfloat16)
    deriv = gll_derivative()
    eye5, eye2 = np.eye(5, dtype=np.float32), np.eye(2, dtype=np.float32)
    d1 = np.zeros((RP, RP), np.float32)
    d2 = np.zeros((RP, RP), np.float32)
    d1[:50, :50] = np.kron(np.kron(deriv, eye5), eye2)
    d2[:50, :50] = np.kron(np.kron(eye5, deriv), eye2)
    h1, l1 = split_bf16(d1)
    h2, l2 = split_bf16(d2)
    grad = np.concatenate(
        [np.concatenate([h1, h1, l1], 1), np.concatenate([h2, h2, l2], 1)], 0
    )
    h1, l1, h2, l2 = h1.T, l1.T, h2.T, l2.T
    div = np.concatenate([h1, h2, h1, h2, l1, l2], 1)
    return synthesis[:, :512], grad, div


def dot(a, b):
    return jnp.dot(a, b, preferred_element_type=F32)


def kernel(
    ny, nz, nb,
    disp_h, rad_h, mod_h, imass_h, cnt_h, sp_h, ro_h, fs_h, ws_h, box_h, speed_h, tsyn_h, grad_h, div_h,
    ga, acc,
    disp, rad, mod, imass, cnt, sp, ro, fs, ws, box, speed, tsyn, gradm, divm,
    field, modf, radf, massf, lhs1, lhs2, pots, tracs, gather, divs,
    edge, edge_in, xin, yout, yin, zout, zin, spot, vals, route, part_in, line, face, face_in,
    in_sem, send_sem, recv_sem, relay_sem,
):
    mer = lax.axis_index("mer")
    grp = lax.axis_index("grp")
    bx = lax.axis_index("box")
    my_y = mer // nz
    my_z = mer % nz
    n_mer = ny * nz
    chain = (mer * 2 + grp) * nb + bx
    n_dev = n_mer * 2 * nb

    def chain_id(d):
        d = (d + n_dev) % n_dev
        return (d // (2 * nb), (d // nb) % 2, d % nb)

    mer_up = ((mer + 1) % n_mer, grp, bx)
    mer_down = ((mer + n_mer - 1) % n_mer, grp, bx)
    box_up = (mer, grp, (bx + 1) % nb)
    box_down = (mer, grp, (bx + nb - 1) % nb)
    other = (mer, 1 - grp, bx)
    next_id = chain_id(chain + 1)
    prev_id = chain_id(chain - 1)
    y_ahead = sorted(range(1, ny), key=lambda k: (-min(k, ny - k), k))
    z_ahead = sorted(range(1, nz), key=lambda k: (-min(k, nz - k), k))
    y_peers = [(((my_y + k) % ny) * nz + my_z, grp, bx) for k in y_ahead]
    z_peers = [(my_y * nz + (my_z + k) % nz, grp, bx) for k in z_ahead]
    reach = nz // 4
    relay_up = (my_y * nz + (my_z + reach) % nz, grp, bx)
    relay_down = (my_y * nz + (my_z + nz - reach) % nz, grp, bx)
    z_near = [z_peers[i] for i, k in enumerate(z_ahead) if min(k, nz - k) <= reach]
    partners = z_near + y_peers + [mer_up, mer_down, box_up, box_down, other, next_id, prev_id]

    barrier = pltpu.get_barrier_semaphore()
    for partner in partners:
        pl.semaphore_signal(barrier, inc=1, device_id=partner, device_id_type=MESH)

    loads = []
    for index, (src, dst) in enumerate(
        [
            (disp_h, disp), (cnt_h, cnt), (rad_h, rad), (grad_h, gradm), (tsyn_h, tsyn), (mod_h, mod), (sp_h, sp),
            (ws_h, ws), (ro_h, ro), (fs_h, fs), (box_h, box), (div_h, divm), (speed_h, speed),
            (imass_h, imass),
        ]
    ):
        copy = pltpu.make_async_copy(src, dst, in_sem.at[index])
        if index < 10:
            copy.start()
        loads.append(copy)
    (l_disp, l_cnt, l_rad, l_grad, l_tsyn, l_mod, l_sp, l_ws, l_ro, l_fs, l_box, l_div, l_speed, l_imass) = loads

    counter = [0]

    def remote(src, dst, partner):
        index = counter[0]
        counter[0] += 1
        copy = pltpu.make_async_remote_copy(
            src_ref=src, dst_ref=dst, send_sem=send_sem.at[index], recv_sem=recv_sem.at[index],
            device_id=partner, device_id_type=MESH,
        )
        copy.start()
        return copy

    lane = lax.broadcasted_iota(jnp.int32, (1, 1024), 1)
    order = lane & 511
    orderf = order.astype(F32)
    sign = (1 - 2 * (order & 1)).astype(BF16)
    row64 = lax.broadcasted_iota(jnp.int32, (RP, 1), 0)

    field[48:RP, :] = jnp.zeros((RP - 48, 1024), F32)
    radf[...] = jnp.ones((RP, 128), F32)
    l_disp.wait()
    for i in range(25):
        field[2 * i : 2 * i + 2, :] = disp[i]
    l_cnt.wait()
    counts = jnp.where((row64 & 1) == 0, cnt[0:1, 0:1], cnt[0:1, 1:2])
    mask = (order < counts).astype(F32)
    f = field[...] * mask
    l_rad.wait()
    for i in range(25):
        radf[2 * i : 2 * i + 2, :] = jnp.broadcast_to(rad[i // 5][:, i % 5 : i % 5 + 1], (2, 128))
    invr = (1.0 / radf[...])[:, 0:1]
    fhi = f.astype(BF16)
    flo = (f - fhi.astype(F32)).astype(BF16)
    l_grad.wait()
    g12 = dot(gradm[...], jnp.concatenate([fhi, flo, fhi], 0)).astype(BF16)
    lhs1[0:128, :] = g12
    lhs1[256:384, :] = g12 * sign
    g3 = (jnp.concatenate([-f[:, 512:], f[:, :512]], 1) * orderf * invr).astype(BF16)
    lhs1[128:192, :] = g3
    lhs1[384:448, :] = g3 * sign
    lhs1[192:256, :] = fhi
    lhs1[448:512, :] = fhi * sign

    l_sp.wait()
    l_ws.wait()
    second = (sp[...] >= 25).astype(jnp.int32)
    point = (sp[...] - 25 * second) * 2 + second
    packed = ((ws[...] >> 7) * RP + point) | ((ws[...] & 127) << 9)
    packed = jnp.broadcast_to(packed, (128, 128)).T
    key = packed & 511
    offset = packed >> 9
    lane128 = lax.broadcasted_iota(jnp.int32, (128, 128), 1)
    for t in range(4):
        cols = slice(t * 128, (t + 1) * 128)
        gather[0:128, cols] = (key == lane128 + t * 128).astype(F32).astype(BF16)
        gather[128:256, cols] = (key + RP == lane128 + t * 128).astype(F32).astype(BF16)

    l_ro.wait()
    l_fs.wait()
    row = lax.broadcasted_iota(jnp.int32, (ny * nz * 8, 128), 0)
    step = row >> 3
    target = (((my_y + step // nz) % ny) * nz + (my_z + step % nz) % nz) * 16 + (row & 7)
    keys = jnp.broadcast_to(ro[...] * 16 + fs[...], (ny * nz * 8, 128))
    route[:, 0:128] = (keys == target).astype(F32).astype(BF16)
    route[:, 128:256] = (keys == target + 8).astype(F32).astype(BF16)

    modf[48:RP, :] = jnp.zeros((RP - 48, 1024), F32)
    l_mod.wait()
    for i in range(25):
        modf[2 * i : 2 * i + 2, :] = mod[i].astype(F32)
    l_tsyn.wait()
    for copy in (l_box, l_div, l_speed, l_imass):
        copy.start()
    for s in range(2):
        half = slice(s * 512, (s + 1) * 512)
        phys = dot(lhs1[s * 256 : (s + 1) * 256, :], tsyn[...])
        for c in range(3):
            lhs2[s * 192 + c * RP : s * 192 + (c + 1) * RP, :] = (modf[:, half] * phys[c * RP : (c + 1) * RP]).astype(BF16)
        for t in range(4):
            b = s * 4 + t
            pots[b * RP : (b + 1) * RP, :] = phys[192:256, t * 128 : (t + 1) * 128].astype(BF16)

    coeffs = lax.dot_general(lhs2[...], tsyn[...], (((1,), (1,)), ((), ())), preferred_element_type=F32)
    scale = mask * jnp.where(order == 0, 1.0 / 1024, 1.0 / 2048)
    signed = scale * (1 - 2 * (order & 1)).astype(F32)
    c1, c2, c3 = (coeffs[c * RP : (c + 1) * RP] * scale + coeffs[192 + c * RP : 256 + c * RP] * signed for c in range(3))

    c2hi = c2.astype(BF16)
    synth = dot(jnp.concatenate([c2hi, c2hi * sign], 0), tsyn[...]).astype(BF16)
    for s in range(2):
        for t in range(4):
            b = s * 4 + t
            tracs[b * RP : (b + 1) * RP, :] = synth[s * RP : (s + 1) * RP, t * 128 : (t + 1) * 128]
    windows = []
    for table in (pots, tracs):
        got = dot(gather[...], table[...])
        windows.append(jnp.where(lane128 >= offset, got[0:128], got[128:256]))
    where = (offset + (lane128 & 31)) & 127
    pieces = [jnp.take_along_axis(window, where, axis=1, mode="promise_in_bounds") for window in windows]
    merged = jnp.where((lane128 & 32) == 0, pieces[0], pieces[1])
    vals[0:128, :] = jnp.where(lane128 < 64, merged, 0.0).astype(BF16)
    vals[128:256, :] = jnp.where(lane128 < 64, 0.0, merged).astype(BF16)
    face[...] = dot(route[...], vals[...]).reshape(ny * nz, 8, 128).astype(BF16)
    pl.semaphore_wait(barrier, len(partners))
    pl.semaphore_signal(relay_sem.at[0], inc=1, device_id=relay_up, device_id_type=MESH)
    pl.semaphore_signal(relay_sem.at[1], inc=1, device_id=relay_down, device_id_type=MESH)
    pieces = [(nz // 4, nz // 2), (0, nz // 4), (3 * nz // 4, nz // 4)]
    part_copies = [
        [
            remote(face.at[pl.ds(step * nz + lo, n)], part_in.at[k, pl.ds(lo, n)], y_peers[k])
            for k, step in enumerate(y_ahead)
        ]
        for lo, n in pieces
    ]
    l_box.wait()
    yout[0:32, :] = box[pl.ds(0, 32, stride=16), :]
    yout[32:64, :] = box[pl.ds(15, 32, stride=16), :]
    far_lane = 127 * (1 - grp)
    near_lane = 127 * grp
    row128 = lax.broadcasted_iota(jnp.int32, (128, 128), 0)
    pick = (row128 == far_lane).astype(F32).astype(BF16)
    column = dot(box[...].astype(BF16), pick).reshape(64, 8, 128)
    block64 = lax.broadcasted_iota(jnp.int32, (64, 1, 128), 0)
    lane64 = lax.broadcasted_iota(jnp.int32, (64, 1, 128), 2)
    place = (block64 >> 1) + (block64 & 1) * 64
    pot_mask = lane64 == place
    trac_mask = lane64 == place + 32
    zout[...] = jnp.sum(jnp.where(pot_mask, column, 0.0), axis=0)
    x_copies = [
        remote(box.at[pl.ds(0, 16)], xin.at[1], mer_down),
        remote(box.at[pl.ds(496, 16)], xin.at[0], mer_up),
    ]
    y_copies = [
        remote(yout.at[pl.ds(0, 32)], yin.at[1], box_down),
        remote(yout.at[pl.ds(32, 32)], yin.at[0], box_up),
    ]
    z_copy = remote(zout, zin, other)

    c1hi = c1.astype(BF16)
    c1lo = (c1 - c1hi.astype(F32)).astype(BF16)
    c2lo = (c2 - c2hi.astype(F32)).astype(BF16)
    l_div.wait()
    div = dot(divm[...], jnp.concatenate([c1hi, c2hi, c1lo, c2lo, c1hi, c2hi], 0))
    div = div + jnp.concatenate([c3[:, 512:], -c3[:, :512]], 1) * orderf * invr
    divs[...] = div
    for k in range(5):
        edge[0, k : k + 1, :] = divs[41 + 2 * k : 42 + 2 * k, :]
        edge[1, k : k + 1, :] = divs[2 * k : 2 * k + 1, :]
    edge[0, 5:8, :] = jnp.zeros((3, 1024), F32)
    edge[1, 5:8, :] = jnp.zeros((3, 1024), F32)
    edge_copies = [
        remote(edge.at[0], edge_in.at[0], next_id),
        remote(edge.at[1], edge_in.at[1], prev_id),
    ]

    l_speed.wait()
    b = box[...]
    row512 = lax.broadcasted_iota(jnp.int32, (512, 128), 0) & 15
    lane512 = lax.broadcasted_iota(jnp.int32, (512, 128), 1)
    zero16 = jnp.zeros((16, 128), F32)
    total = jnp.concatenate([zero16, b[:-16]], 0) + jnp.concatenate([b[16:], zero16], 0)
    total = total + jnp.where(row512 == 0, 0.0, pltpu.roll(b, 1, 0)) + jnp.where(row512 == 15, 0.0, pltpu.roll(b, 511, 0))
    total = total + jnp.where(lane512 == 0, 0.0, pltpu.roll(b, 1, 1)) + jnp.where(lane512 == 127, 0.0, pltpu.roll(b, 127, 1))
    acc[...] = speed[...] * (total - 6.0 * b)

    face_copies = []
    for (lo, n), copies in zip(pieces, part_copies):
        part = face[lo : lo + n].astype(F32)
        for k, copy in enumerate(copies):
            copy.wait_recv()
            part = part + part_in[k, lo : lo + n].astype(F32)
        line[lo : lo + n] = part.astype(BF16)
        if lo == 0:
            own = part[0]
        if not face_copies:
            pl.semaphore_wait(relay_sem.at[0], 1)
            pl.semaphore_wait(relay_sem.at[1], 1)
        for k, step in enumerate(z_ahead):
            if lo <= step < lo + n:
                face_copies.append(remote(line.at[step], face_in.at[k], z_peers[k]))

    for copy in x_copies + y_copies + [z_copy]:
        copy.wait_recv()
    acc[0:16, :] += speed[0:16, :] * jnp.where(mer == 0, 0.0, xin[0])
    acc[496:512, :] += speed[496:512, :] * jnp.where(mer == n_mer - 1, 0.0, xin[1])
    acc[pl.ds(0, 32, stride=16), :] += speed[pl.ds(0, 32, stride=16), :] * jnp.where(bx == 0, 0.0, yin[0])
    acc[pl.ds(15, 32, stride=16), :] += speed[pl.ds(15, 32, stride=16), :] * jnp.where(bx == nb - 1, 0.0, yin[1])
    lane128 = lax.broadcasted_iota(jnp.int32, (128, 128), 1)
    far = (lane128 == far_lane).astype(F32).astype(BF16)
    spread = jnp.where(pot_mask, zin[...][None], 0.0).reshape(512, 128)
    acc[...] += speed[...] * dot(spread.astype(BF16), far)

    l_imass.wait()
    for i in range(25):
        massf[2 * i : 2 * i + 2, :] = jnp.broadcast_to(imass[i // 5][:, i % 5 : i % 5 + 1], (2, 128))
    for copy in edge_copies:
        copy.wait_recv()
    for k in range(5):
        inner = divs[40 + 2 * k : 41 + 2 * k, :] + divs[1 + 2 * k : 2 + 2 * k, :]
        divs[40 + 2 * k : 41 + 2 * k, :] = inner
        divs[1 + 2 * k : 2 + 2 * k, :] = inner
        divs[2 * k : 2 * k + 1, :] += jnp.where(chain == 0, 0.0, edge_in[0, k : k + 1, :])
        divs[41 + 2 * k : 42 + 2 * k, :] += jnp.where(chain == n_dev - 1, 0.0, edge_in[1, k : k + 1, :])
    for i in range(25):
        ga[i] = divs[2 * i : 2 * i + 2, :] * -massf[2 * i : 2 * i + 2, 0:1]

    both_mask = pot_mask | trac_mask
    row256 = lax.broadcasted_iota(jnp.int32, (256, 256), 0)
    col256 = lax.broadcasted_iota(jnp.int32, (256, 256), 1)
    keep = ((row256 & 32) == 0) == (col256 < 128)
    spot[...] = (keep & ((col256 & 127) == near_lane)).astype(F32).astype(BF16)
    for copy in x_copies + y_copies + [z_copy] + sum(part_copies, []) + edge_copies + face_copies:
        copy.wait_send()
    cut = len(face_copies) // 2
    mine = own
    for first, last in ((cut, len(face_copies)), (0, cut)):
        if first < last:
            for k in range(last - 1, first - 1, -1):
                face_copies[k].wait_recv()
            mine = mine + jnp.sum(face_in[first:last].astype(F32), axis=0)
    hi = mine.astype(BF16).astype(F32)
    lo = mine - hi
    hi = jnp.where(both_mask, hi[None], 0.0).reshape(512, 128).astype(BF16)
    lo = jnp.where(both_mask, lo[None], 0.0).reshape(512, 128).astype(BF16)
    sides = dot(jnp.concatenate([hi, lo], 1), spot[...])
    acc[...] += speed[...] * sides[:, :128] + 0.25 * sides[:, 128:]


def write_out(ga, ba, ga_h, ba_h, sem):
    copies = [pltpu.make_async_copy(ga, ga_h, sem.at[0]), pltpu.make_async_copy(ba, ba_h, sem.at[1])]
    for copy in copies:
        copy.start()
    for copy in copies:
        copy.wait()


def shards(ny, nz, nb, displacement, radius, bulk, imass, counts, source, owner, slot, window, box, speed):
    tsyn, grad, div = constants()
    args = [
        displacement.transpose(1, 2, 0, 3).reshape(25, 2, 1024),
        radius.transpose(1, 0, 2),
        bulk.transpose(1, 2, 0, 3).reshape(25, 2, 1024),
        imass.transpose(1, 0, 2),
        counts.reshape(1, 2),
        source.reshape(1, NREC),
        owner.reshape(1, NREC),
        slot.reshape(1, NREC),
        window.reshape(1, NREC),
        box.reshape(512, 128),
        speed.reshape(512, 128),
        jnp.asarray(tsyn), jnp.asarray(grad), jnp.asarray(div),
    ]
    n_copies = 5 + 2 + 3 * (ny - 1) + nz - 1
    hbm = pl.BlockSpec(memory_space=pltpu.HBM)
    vmem = pltpu.VMEM
    scratch = [vmem(a.shape, a.dtype) for a in args] + [
        vmem((RP, 1024), F32),
        vmem((RP, 1024), F32),
        vmem((RP, 128), F32),
        vmem((RP, 128), F32),
        vmem((512, 1024), BF16),
        vmem((384, 512), BF16),
        vmem((512, 128), BF16),
        vmem((512, 128), BF16),
        vmem((256, 512), BF16),
        vmem((RP, 1024), F32),
        vmem((2, 8, 1024), F32),
        vmem((2, 8, 1024), F32),
        vmem((2, 16, 128), F32),
        vmem((64, 128), F32),
        vmem((2, 32, 128), F32),
        vmem((8, 128), F32),
        vmem((8, 128), F32),
        vmem((256, 256), BF16),
        vmem((256, 128), BF16),
        vmem((ny * nz * 8, 256), BF16),
        vmem((ny - 1, nz, 8, 128), BF16),
        vmem((nz, 8, 128), BF16),
        vmem((ny * nz, 8, 128), BF16),
        vmem((nz - 1, 8, 128), BF16),
        pltpu.SemaphoreType.DMA((14,)),
        pltpu.SemaphoreType.DMA((n_copies,)),
        pltpu.SemaphoreType.DMA((n_copies,)),
        pltpu.SemaphoreType.REGULAR((2,)),
    ]
    ga, ba = pl.pallas_call(
        functools.partial(kernel, ny, nz, nb),
        out_shape=(vmem((25, 2, 1024), F32), vmem((512, 128), F32)),
        in_specs=[hbm] * len(args),
        out_specs=(pl.BlockSpec(memory_space=vmem),) * 2,
        scratch_shapes=scratch,
        compiler_params=pltpu.CompilerParams(
            collective_id=0, has_side_effects=True, vmem_limit_bytes=40 * 2**20
        ),
        name="step",
    )(*[pltpu.with_memory_space_constraint(a, pltpu.HBM) for a in args])
    ga, ba = pl.pallas_call(
        write_out,
        out_shape=(jax.ShapeDtypeStruct((25, 2, 1024), F32), jax.ShapeDtypeStruct((512, 128), F32)),
        in_specs=[pl.BlockSpec(memory_space=vmem)] * 2,
        out_specs=(hbm, hbm),
        scratch_shapes=[pltpu.SemaphoreType.DMA((2,))],
        name="write_out",
    )(pltpu.with_memory_space_constraint(ga, vmem), pltpu.with_memory_space_constraint(ba, vmem))
    ga = ga.reshape(5, 5, 2, 1024).transpose(2, 0, 1, 3)
    return ga, ba.reshape(32, 16, 128)


def solution(mesh):
    n_mer = mesh.shape["mer"]
    nz = NZ_FULL if n_mer == 64 else 4
    d = P(("mer", "grp", "box"))
    return jax.shard_map(
        functools.partial(shards, n_mer // nz, nz, mesh.shape["box"]),
        mesh=mesh,
        in_specs=(d, d, d, d, d, d, d, d, d, P("mer", "box", "grp"), P("mer", "box", "grp")),
        out_specs=(d, P("mer", "box", "grp")),
        check_vma=False,
    )
```
